256 devices in a mesh: seq: 64 (over y, z, x_lo), tp: 4 (over x_hi, core).
Axes of the slice: x: 4 (x_hi: 2, x_lo: 2; x = x_hi * 2 + x_lo), y: 4, z: 8, core: 2. Of those that a mesh axis runs over, the one named last changes fastest.
Arguments:
- token_ids: int32 [8192], P('seq'), may hold values from 0 to 511
- embedding: bfloat16 [512, 8192], P(None, 'tp'), may hold values from -800 to 800
- norm_gain: float32 [8192], P('tp'), may hold values from 0.1 to 1.9
- projection: bfloat16 [8192, 3, 8192], P('tp', None, 'seq'), may hold values from -0.0625 to 0.0625
- short_filter: float32 [3, 3, 8192], replicated, may hold values from -3.5 to 3.5
- residues: float32 [8192, 16], replicated, may hold values from -1.8 to 1.8
- decay_rates: float32 [8192, 16], replicated, may hold values from 6.1035156e-05 to 0.04
Outputs:
- hyena_out: bfloat16 [8192, 8192], P(('seq', 'tp'))
The draws below stay inside these ranges and needn't reach their ends.
Inputs may be any that keep to these rules, and one draw needn't show every extreme that they name: `token_ids`: ids of a 512-entry vocabulary.
All inputs are finite; a program needn't handle non-finite values.
Results may differ from the reference program's by a relative error of at most 0.0079.
Values may be sent and summed in bfloat16 or wider, within the bound.
A program may use at most 128 MiB of HBM per device.

```python
import math
import jax
import jax.numpy as jnp
import numpy as np
from jax import lax

D = 8192
V = 512
K = 16
TAPS = 3
TOKENS = 8192


def draw_embedding(key, part):
    key = jax.random.fold_in(key, 11)
    key_base, key_rows = jax.random.split(key, 2)
    column = jnp.arange(D, dtype=jnp.float32) / D
    row_scale = 10.0 ** jax.random.uniform(key_rows, (V, 1), jnp.float32)
    base_draw = jnp.clip(jax.random.normal(key_base, (V, D), jnp.float32), -5.0, 5.0)
    values = base_draw * (10.0 ** column)[None, :] * row_scale
    return values.astype(jnp.bfloat16)


def with_ends(drawn, own_key, low, top_value):
    dims = drawn.shape
    index_at = [jax.random.randint(jax.random.fold_in(own_key, axis), (), 0, dims[axis]) for axis in range(len(dims))]
    drawn = drawn.at[tuple(index_at)].set(low)
    longest = dims.index(max(dims))
    index_at[longest] = (index_at[longest] + 1) % dims[longest]
    return drawn.at[tuple(index_at)].set(top_value)


def shard_levels(rng, extent, pieces, smallest, largest):
    gain = 1.0
    for dim, parts in pieces:
        heights = jax.random.uniform(jax.random.fold_in(jax.random.fold_in(rng, 6), dim), (parts,), jnp.float32, smallest / len(pieces), largest / len(pieces))
        gain = gain * jnp.repeat(jnp.exp(heights), extent[dim] // parts).reshape((-1,) + (1,) * (len(extent) - 1 - dim))
    return gain


def cumulative_ranks(amount, slope):
    weights = [(1 << 20) // math.isqrt(grade ** slope) + 1 for grade in range(1, amount + 1)]
    scale = 1 + sum(weights) // (1 << 30)
    return np.cumsum(np.array([max(1, weight // scale) for weight in weights]))


def skewed_ids(key, shape, count, lean):
    listing = cumulative_ranks(count, lean)
    ticket = jax.random.randint(jax.random.fold_in(key, 1), shape, 0, int(listing[count - 1]))
    rank = jnp.searchsorted(jnp.asarray(listing, jnp.int32), ticket, side="right")
    return jax.random.permutation(jax.random.fold_in(key, 2), count)[rank].astype(jnp.int32)


def centred(stream_key, dims, spread, reach, pieces=(), kind=jnp.bfloat16):
    values = spread * jax.random.normal(stream_key, dims, jnp.float32)
    if pieces:
        values = values * shard_levels(stream_key, dims, pieces, -0.22, 0.18)
    return jnp.clip(values, -reach, reach).astype(kind)


def setup_inputs(seed: int = 0) -> dict:
    key_list = jax.random.split(jax.random.key(seed), 8)
    token_ids = with_ends(skewed_ids(key_list[0], (TOKENS,), V, 1), jax.random.fold_in(key_list[0], 3), 0, V - 1).astype(jnp.int32)
    embedding = draw_embedding(jax.random.fold_in(key_list[7], 71), 0)
    norm_gain = jnp.clip(1.0 + 0.18 * jax.random.normal(key_list[2], (D,), jnp.float32), 0.1, 1.9)
    projection = centred(key_list[3], (D, 3, D), D ** -0.5, 0.0625, ((0, 4), (2, 64)))
    short_filter = centred(key_list[4], (3, TAPS, D), TAPS ** -0.5, 3.5, (), jnp.float32)
    residues = centred(key_list[5], (D, K), 0.3, 1.8, (), jnp.float32)
    decay_rates = jnp.clip(jnp.exp(jax.random.uniform(key_list[6], (D, K), jnp.float32, math.log(6.103515625e-05), math.log(0.04))), 6.103515625e-05, 0.04)
    return dict(token_ids=token_ids, embedding=embedding, norm_gain=norm_gain, projection=projection, short_filter=short_filter, residues=residues, decay_rates=decay_rates)


def long_conv(gated_in, decay_rates, residues):
    decay = jnp.exp(-decay_rates)
    mode_weight = residues * jnp.sqrt(-jnp.expm1(-2.0 * decay_rates))

    def advance(state, column):
        state = decay * state + column[:, None]
        return (state, lax.optimization_barrier(jnp.sum(mode_weight * state, axis=1)))
    initial = jnp.zeros(decay_rates.shape, jnp.float32)
    _, outputs = lax.scan(advance, initial, gated_in)
    return outputs

def reference(token_ids, embedding, norm_gain, projection, short_filter, residues, decay_rates):
    features = embedding.astype(jnp.float32)
    energy = lax.optimization_barrier(jnp.mean(features * features, axis=1, keepdims=True))
    normed = (features * lax.rsqrt(energy + 1e-05) * norm_gain[None, :]).astype(jnp.bfloat16)
    group_width = D // 8
    results = []
    for group_index in range(8):
        col_first = group_index * group_width
        col_last = col_first + group_width
        lookup_table = jnp.stack([jnp.dot(normed, projection[:, stream, col_first:col_last], preferred_element_type=jnp.float32) for stream in range(3)]).astype(jnp.bfloat16)
        lookup_table = lax.optimization_barrier(lookup_table)
        streams = lookup_table[:, token_ids, :]
        padded = jnp.pad(streams, ((0, 0), (TAPS - 1, 0), (0, 0)))
        filtered = jnp.zeros((3, TOKENS, group_width), jnp.float32)
        for tap_index in range(TAPS):
            lag_start = TAPS - 1 - tap_index
            filtered = filtered + short_filter[:, tap_index, col_first:col_last][:, None, :] * padded[:, lag_start:lag_start + TOKENS, :].astype(jnp.float32)
        gated_in = lax.optimization_barrier((filtered[1] * filtered[2]).astype(jnp.bfloat16))
        long_out = long_conv(gated_in.astype(jnp.float32), decay_rates[col_first:col_last], residues[col_first:col_last])
        results.append(jnp.transpose((filtered[0] * long_out).astype(jnp.bfloat16)))
    return jnp.concatenate(results, axis=0)
```

```python
import functools

import jax
import jax.numpy as jnp
from jax import lax
from jax.experimental import pallas as pl
from jax.experimental.pallas import tpu as pltpu
from jax.sharding import PartitionSpec as P

MESH = pl.DeviceIdType.MESH
F32 = jnp.float32
BF16 = jnp.bfloat16
LANES = 128
CHANNELS = 32
MODES = 16
STREAMS = 3
TAPS = 3
VOCAB = 512
HALF = 256
ORDER = (1, 2, 0)


def split(x):
    hi = x.astype(BF16)
    return hi, (x - hi.astype(F32)).astype(BF16)


def quad_operands(x):
    hi = x.astype(BF16).astype(F32)
    lo = x - hi
    lane = lax.broadcasted_iota(jnp.int32, x.shape, 1)
    low = lane < 64
    first = jnp.where(low, hi, pltpu.roll(lo, 64, 1))
    second = jnp.where(low, pltpu.roll(hi, 64, 1), lo)
    hi = hi.astype(BF16)
    return (
        jnp.concatenate([first.astype(BF16), hi], axis=1),
        jnp.concatenate([second.astype(BF16), hi], axis=1),
    )


def kernel(
    model_width,
    seq_count,
    emb_hbm,
    gain_hbm,
    proj_hbm,
    ids_hbm,
    filt_hbm,
    res_hbm,
    rate_hbm,
    obuf,
    emb,
    gain,
    proj,
    ids,
    filt,
    res,
    rate,
    wproj,
    part,
    recv1,
    own,
    send2,
    recv2,
    en_part,
    en_own,
    en_recv1,
    en_sum,
    en_recv2,
    tblkv,
    tblq,
    onehot,
    taps,
    weights,
    lquad,
    colw,
    step_rate,
    gated,
    qfilt,
    yintra,
    ends,
    carries,
    ybuf,
    load_sem,
    id_send,
    id_recv,
    s1_send,
    s1_recv,
    s2_send,
    s2_recv,
    e_send,
    e_recv,
):
    seq = lax.axis_index("seq")
    tp = lax.axis_index("tp")
    core = lax.rem(tp, 2)
    far = tp // 2
    sibling = tp + 1 - 2 * core
    across_tp = lax.rem(tp + 2, 4)

    barrier = pltpu.get_barrier_semaphore()
    for peer in (sibling, across_tp):
        pl.semaphore_signal(barrier, inc=1, device_id={"seq": seq, "tp": peer}, device_id_type=MESH)

    def greet(n, _):
        peer = lax.rem(seq + n, seq_count)
        pl.semaphore_signal(barrier, inc=1, device_id={"seq": peer, "tp": tp}, device_id_type=MESH)
        return 0

    lax.fori_loop(1, seq_count, greet, 0)

    rows = emb_hbm.shape[0] // 4
    chan0 = pl.multiple_of(seq * LANES, LANES)
    loads = {}

    def load(name, slot, src, dst):
        loads[name] = pltpu.make_async_copy(src, dst, load_sem.at[slot])
        loads[name].start()

    load("gain", 1, gain_hbm, gain)
    load("proj1", 2, proj_hbm.at[1], proj.at[1])
    for r in range(4):
        load(f"emb{r}", 3 + r, emb_hbm.at[pl.ds(r * rows, rows), :], emb.at[pl.ds(r * rows, rows), :])
    load("ids", 0, ids_hbm, ids.at[seq])
    load("proj2", 7, proj_hbm.at[2], proj.at[2])
    load("proj0", 8, proj_hbm.at[0], proj.at[0])
    load("rate", 9, rate_hbm.at[:, pl.ds(chan0, LANES)], rate)
    load("res", 10, res_hbm.at[:, pl.ds(chan0, LANES)], res)
    load("filt", 11, filt_hbm.at[:, :, pl.ds(chan0, LANES)], filt)

    def ids_copy(n):
        return pltpu.make_async_remote_copy(
            src_ref=ids.at[seq], dst_ref=ids.at[seq],
            send_sem=id_send.at[n], recv_sem=id_recv.at[n],
            device_id={"seq": lax.rem(seq + n, seq_count), "tp": tp}, device_id_type=MESH,
        )

    def send_ids(n, _):
        ids_copy(n).start()
        return 0

    def gained(s):
        loads[f"proj{s}"].wait()

        def one(k, _):
            start = pl.multiple_of(k * LANES, LANES)
            row = gain[pl.ds(k, 1), :]
            column = jnp.transpose(jnp.broadcast_to(row, (LANES, LANES)))
            hi, lo = split(proj[s, pl.ds(start, LANES), :].astype(F32) * column)
            wproj[s, pl.ds(start, LANES), :] = jnp.concatenate([hi, lo], axis=1)
            return 0

        lax.fori_loop(0, proj.shape[1] // LANES, one, 0, unroll=2)

    def project(s, first):
        for r in range(4):
            if first:
                loads[f"emb{r}"].wait()
            block = emb[pl.ds(r * rows, rows), :]
            both = jnp.dot(block, wproj[s], preferred_element_type=F32)
            turned = jnp.transpose(both[:, :LANES] + both[:, LANES:])
            for q in range(4):
                piece = turned[q * CHANNELS:(q + 1) * CHANNELS, :]
                part[s, q % 2, q // 2, :, r * rows:(r + 1) * rows] = piece

    def send_sibling(s):
        copy = pltpu.make_async_remote_copy(
            src_ref=part.at[s, 1 - core], dst_ref=recv1.at[s],
            send_sem=s1_send.at[s], recv_sem=s1_recv.at[s],
            device_id={"seq": seq, "tp": sibling}, device_id_type=MESH,
        )
        copy.start()
        return copy

    def send_across(s, copy):
        copy.wait_recv()
        send2[s] = part[s, core, 1 - far] + recv1[s, 1 - far]
        after = pltpu.make_async_remote_copy(
            src_ref=send2.at[s], dst_ref=recv2.at[s],
            send_sem=s2_send.at[s], recv_sem=s2_recv.at[s],
            device_id={"seq": seq, "tp": across_tp}, device_id_type=MESH,
        )
        after.start()
        own[s] = part[s, core, far] + recv1[s, far]
        return after

    def energies():
        for r in range(4):
            block = emb[pl.ds(r * rows, rows), :]
            total = jnp.zeros((rows, LANES), F32)
            for k in range(emb.shape[1] // LANES):
                piece = block[:, k * LANES:(k + 1) * LANES].astype(F32)
                total = total + piece * piece
            en_part[pl.ds(r, 1), :] = jnp.sum(jnp.transpose(total), axis=0, keepdims=True)

    def send_energy(step, src, dst, peer):
        copy = pltpu.make_async_remote_copy(
            src_ref=src, dst_ref=dst, send_sem=e_send.at[step], recv_sem=e_recv.at[step],
            device_id={"seq": seq, "tp": peer}, device_id_type=MESH,
        )
        copy.start()
        return copy

    loads["gain"].wait()
    gained(1)
    project(1, True)
    gained(2)
    project(2, False)
    loads["ids"].wait()

    pl.semaphore_wait(barrier, seq_count + 1)
    lax.fori_loop(1, seq_count, send_ids, 0)
    sib = {1: send_sibling(1), 2: send_sibling(2)}
    energies()
    energy1 = send_energy(0, en_part, en_recv1, sibling)
    cross = {1: send_across(1, sib[1]), 2: send_across(2, sib[2])}
    gained(0)
    project(0, False)
    sib[0] = send_sibling(0)
    energy1.wait_recv()
    en_sum[...] = en_part[...] + en_recv1[...]
    energy2 = send_energy(1, en_sum, en_recv2, across_tp)
    cross[0] = send_across(0, sib[0])

    loads["rate"].wait()
    loads["res"].wait()
    loads["filt"].wait()
    turn = lax.rem(LANES - tp * CHANNELS, LANES)
    rates = pltpu.roll(rate[...], turn, 1)
    twice = 2.0 * rates
    series = twice * (
        1.0 - twice / 2 * (1.0 - twice / 3 * (1.0 - twice / 4 * (1.0 - twice / 5 * (1.0 - twice / 6))))
    )
    lost = jnp.where(twice < 0.125, series, 1.0 - jnp.exp(-twice))
    mode = pltpu.roll(res[...], turn, 1) * jnp.sqrt(lost)
    lane16 = lax.broadcasted_iota(jnp.int32, (MODES, LANES), 1).astype(F32)
    lquad[...] = jnp.zeros(lquad.shape, BF16)
    for c in range(CHANNELS):
        rate_c = jnp.broadcast_to(rates[:, c:c + 1], (MODES, LANES))
        mode_c = jnp.broadcast_to(mode[:, c:c + 1], (MODES, LANES))
        hi, lo = split(mode_c * jnp.exp(-rate_c * (lane16 + 1.0)))
        colw[pl.ds(c * MODES, MODES), :] = rate_c
        quad, at = c // 4, c % 4
        cols = pl.ds(at * LANES, LANES)
        lquad[quad, pl.ds(at * MODES, MODES), cols] = hi
        lquad[quad, pl.ds(64 + at * MODES, MODES), cols] = hi
        lquad[quad, pl.ds(128 + 64 * (quad % 2) + at * MODES, MODES), cols] = lo
    row_at = lax.broadcasted_iota(jnp.int32, (LANES, LANES), 0)
    lane_at = lax.broadcasted_iota(jnp.int32, (LANES, LANES), 1)
    behind = (LANES - 1 - row_at).astype(F32)
    keep = lane_at >= row_at

    def operators(g, _):
        start = pl.multiple_of(g * LANES, LANES)
        rate_row = jnp.transpose(colw[pl.ds(start, LANES), :])
        step_rate[g] = rate_row[:8, :] * LANES
        decays = jnp.exp(-rate_row * behind)
        e_hi, e_lo = split(decays)
        grown = quad_operands(jnp.exp(rate_row * (row_at + 1).astype(F32)))
        for half in range(2):
            kernels = jnp.dot(grown[half], lquad[g * 2 + half], preferred_element_type=F32)
            for at in range(4):
                inner = jnp.where(keep, kernels[:, at * LANES:(at + 1) * LANES], 0.0)
                t_hi, t_lo = split(inner)
                c_in = half * 4 + at
                mine = (lane_at >= c_in * MODES) & (lane_at < (c_in + 1) * MODES)
                zero = jnp.zeros((LANES, LANES), F32)
                m_hi = jnp.where(mine, e_hi.astype(F32), zero).astype(BF16)
                m_lo = jnp.where(mine, e_lo.astype(F32), zero).astype(BF16)
                c = g * 8 + c_in
                weights[c, pl.ds(0, LANES), :] = jnp.concatenate([t_hi, m_hi], axis=1)
                weights[c, pl.ds(LANES, LANES), :] = jnp.concatenate([t_lo, m_lo], axis=1)
        return 0

    lax.fori_loop(0, 4, operators, 0)

    for s in range(STREAMS):
        moved = pltpu.roll(filt[s], turn, 1)
        columns = jnp.transpose(jnp.concatenate([moved, jnp.zeros((LANES - TAPS, LANES), F32)], axis=0))
        for j in range(TAPS):
            taps[s * TAPS + j] = jnp.broadcast_to(columns[:CHANNELS, j:j + 1], (CHANNELS, LANES))

    row_of = lax.broadcasted_iota(jnp.int32, (HALF, LANES), 0)

    def mark(slot):
        low = jnp.broadcast_to(ids[slot] & (HALF - 1), (HALF, LANES))
        onehot[slot] = jnp.where(row_of == low, 1.0, 0.0).astype(BF16)

    def arrive(n, _):
        ids_copy(n).wait_recv()
        mark(lax.rem(seq + seq_count - n, seq_count))
        return 0

    mark(seq)
    lax.fori_loop(1, seq_count, arrive, 0)

    energy2.wait_recv()
    scale = lax.rsqrt((en_sum[...] + en_recv2[...]) / model_width + 1e-05)

    def tabulate(s, place, table):
        cross[s].wait_recv()
        height = table.shape[0] // 2
        for q in range(4):
            lanes = pl.ds(q * LANES, LANES)
            value = (own[s, :, lanes] + recv2[s, :, lanes]) * scale[q:q + 1, :]
            table[pl.ds((q // 2) * height + place * CHANNELS, CHANNELS), pl.ds((q % 2) * LANES, LANES)] = value.astype(BF16)

    def filter_streams(table, streams, unroll, emit):
        height = table.shape[0] // 2
        lane = lax.broadcasted_iota(jnp.int32, (height, LANES), 1)
        first_lane = lane < 1
        first_two = lane < 2

        def pair(i, carry):
            before1, before2 = carry
            hot = jnp.concatenate([onehot[2 * i], onehot[2 * i + 1]], axis=1)
            both = jnp.dot(table[...], hot, preferred_element_type=F32)
            for u in range(2):
                j = 2 * i + u
                upper = jnp.broadcast_to(ids[j], (height, LANES)) >= HALF
                lanes = slice(u * LANES, (u + 1) * LANES)
                now = jnp.where(upper, both[height:, lanes], both[:height, lanes])
                one, two = pltpu.roll(now, 1, 1), pltpu.roll(now, 2, 1)
                back1 = jnp.where(first_lane, before1, one)
                back2 = jnp.where(first_two, before2, two)
                before1, before2 = one, two
                filtered = []
                for place, s in enumerate(streams):
                    mine = slice(place * CHANNELS, (place + 1) * CHANNELS)
                    filtered.append(
                        taps[s * TAPS] * now[mine] + taps[s * TAPS + 1] * back1[mine] + taps[s * TAPS + 2] * back2[mine]
                    )
                emit(pl.ds(pl.multiple_of(j * CHANNELS, CHANNELS), CHANNELS), *filtered)
            return before1, before2

        nothing = jnp.zeros((height, LANES), F32)
        lax.fori_loop(0, seq_count // 2, pair, (nothing, nothing), unroll=unroll)

    def emit_gated(at, k, v):
        gated[at, :] = (k * v).astype(BF16).astype(F32)

    def emit_query(at, q):
        qfilt[at, :] = q

    tabulate(1, 0, tblkv)
    tabulate(2, 1, tblkv)
    filter_streams(tblkv, (1, 2), 8, emit_gated)
    tabulate(0, 0, tblq)
    filter_streams(tblq, (0,), 8, emit_query)

    def inside(g, _):
        total = jnp.zeros((seq_count, LANES), F32)
        for at in range(8):
            c = g * 8 + at
            x = gated[pl.ds(c, seq_count, stride=CHANNELS), :].astype(BF16)
            result = jnp.dot(jnp.concatenate([x, x], axis=1), weights[c], preferred_element_type=F32)
            yintra[c] = result[:, :LANES]
            total = total + result[:, LANES:]
        ends[g] = total
        return 0

    lax.fori_loop(0, 4, inside, 0)

    sub = lax.broadcasted_iota(jnp.int32, (8, LANES), 0)
    for g in range(4):
        rate_row = step_rate[g]
        own_decay = jnp.exp(-rate_row * sub.astype(F32))
        eighth = jnp.exp(-rate_row * 8.0)
        factors = [(d, jnp.where(sub >= d, jnp.exp(-rate_row * float(d)), 0.0)) for d in (1, 2, 4)]
        entering = jnp.zeros((8, LANES), F32)
        for v in range(seq_count // 8):
            span = ends[g, pl.ds(v * 8, 8), :]
            for d, factor in factors:
                span = span + factor * pltpu.roll(span, d, 0)
            shifted = jnp.where(sub >= 1, pltpu.roll(span, 1, 0), 0.0)
            carries[g, pl.ds(v * 8, 8), :] = shifted + own_decay * entering
            entering = jnp.broadcast_to(span[7:8, :], (8, LANES)) + eighth * entering

    def across(g, _):
        operands = quad_operands(carries[g])
        for half in range(2):
            result = jnp.dot(operands[half], lquad[g * 2 + half], preferred_element_type=F32)
            for at in range(4):
                c = g * 8 + half * 4 + at
                ybuf[pl.ds(c, seq_count, stride=CHANNELS), :] = yintra[c] + result[:, at * LANES:(at + 1) * LANES]
        return 0

    lax.fori_loop(0, 4, across, 0)

    def gate(j, _):
        at = pl.ds(pl.multiple_of(j * CHANNELS, CHANNELS), CHANNELS)
        obuf[:, pl.ds(pl.multiple_of(j * LANES, LANES), LANES)] = (qfilt[at, :] * ybuf[at, :]).astype(BF16)
        return 0

    lax.fori_loop(0, seq_count, gate, 0, unroll=4)

    def sent_ids(n, _):
        ids_copy(n).wait_send()
        return 0

    lax.fori_loop(1, seq_count, sent_ids, 0)
    for copy in list(sib.values()) + list(cross.values()) + [energy1, energy2]:
        copy.wait_send()


def on_device(token_ids, embedding, norm_gain, projection, short_filter, residues, decay_rates):
    seq_count = lax.axis_size("seq")
    vocab, features = embedding.shape
    model_width = short_filter.shape[2]
    tokens = seq_count * LANES
    hbm = pl.BlockSpec(memory_space=pltpu.HBM)
    dma = pltpu.SemaphoreType.DMA
    vmem = pltpu.VMEM
    scratch = [
        vmem((vocab, features), BF16),
        vmem((features // LANES, LANES), F32),
        vmem((STREAMS, features, LANES), BF16),
        vmem((seq_count, 1, LANES), jnp.int32),
        vmem((STREAMS, TAPS, LANES), F32),
        vmem((MODES, LANES), F32),
        vmem((MODES, LANES), F32),
        vmem((STREAMS, features, 2 * LANES), BF16),
        vmem((STREAMS, 2, 2, CHANNELS, vocab), F32),
        vmem((STREAMS, 2, CHANNELS, vocab), F32),
        vmem((STREAMS, CHANNELS, vocab), F32),
        vmem((STREAMS, CHANNELS, vocab), F32),
        vmem((STREAMS, CHANNELS, vocab), F32),
        vmem((4, LANES), F32),
        vmem((4, LANES), F32),
        vmem((4, LANES), F32),
        vmem((4, LANES), F32),
        vmem((4, LANES), F32),
        vmem((4 * CHANNELS, HALF), BF16),
        vmem((2 * CHANNELS, HALF), BF16),
        vmem((seq_count, HALF, LANES), BF16),
        vmem((STREAMS * TAPS, CHANNELS, LANES), F32),
        vmem((CHANNELS, 2 * LANES, 2 * LANES), BF16),
        vmem((8, 2 * LANES, 4 * LANES), BF16),
        vmem((CHANNELS * MODES, LANES), F32),
        vmem((4, 8, LANES), F32),
        vmem((seq_count * CHANNELS, LANES), F32),
        vmem((seq_count * CHANNELS, LANES), F32),
        vmem((CHANNELS, seq_count, LANES), F32),
        vmem((4, seq_count, LANES), F32),
        vmem((4, seq_count, LANES), F32),
        vmem((seq_count * CHANNELS, LANES), F32),
        dma((12,)),
        dma((seq_count,)),
        dma((seq_count,)),
        dma((STREAMS,)),
        dma((STREAMS,)),
        dma((STREAMS,)),
        dma((STREAMS,)),
        dma((2,)),
        dma((2,)),
    ]
    return pl.pallas_call(
        functools.partial(kernel, model_width, seq_count),
        out_shape=vmem((CHANNELS, tokens), BF16),
        in_specs=[hbm] * 7,
        out_specs=pl.BlockSpec(memory_space=vmem),
        scratch_shapes=scratch,
        compiler_params=pltpu.CompilerParams(
            collective_id=0, has_side_effects=True, vmem_limit_bytes=56 * 1024 * 1024
        ),
    )(
        embedding,
        norm_gain.reshape(features // LANES, LANES),
        jnp.transpose(projection, (1, 0, 2)),
        token_ids.reshape(1, LANES),
        short_filter,
        jnp.transpose(residues),
        jnp.transpose(decay_rates),
    )


def solution(mesh):
    return jax.shard_map(
        on_device,
        mesh=mesh,
        in_specs=(P("seq"), P(None, "tp"), P("tp"), P("tp", None, "seq"), P(), P(), P()),
        out_specs=P(("seq", "tp"), None),
        check_vma=False,
    )
```

```python
import functools
import math

import jax
import jax.numpy as jnp
from jax import lax
from jax.experimental import pallas as pl
from jax.experimental.pallas import tpu as pltpu
from jax.sharding import PartitionSpec as P

MESH = pl.DeviceIdType.MESH
F32 = jnp.float32
BF16 = jnp.bfloat16
LANES = 128
CHANNELS = 32
MODES = 16
STREAMS = 3
TAPS = 3
VOCAB = 512
HALF = 256
ORDER = (1, 2, 0)


def split(x):
    hi = x.astype(BF16)
    return hi, (x - hi.astype(F32)).astype(BF16)


def quad_operands(x):
    hi = x.astype(BF16).astype(F32)
    lo = x - hi
    lane = lax.broadcasted_iota(jnp.int32, x.shape, 1)
    low = lane < 64
    first = jnp.where(low, hi, pltpu.roll(lo, 64, 1))
    second = jnp.where(low, pltpu.roll(hi, 64, 1), lo)
    hi = hi.astype(BF16)
    return (
        jnp.concatenate([first.astype(BF16), hi], axis=1),
        jnp.concatenate([second.astype(BF16), hi], axis=1),
    )


def kernel(
    model_width,
    seq_count,
    emb_hbm,
    gain_hbm,
    proj_hbm,
    ids_hbm,
    filt_hbm,
    res_hbm,
    rate_hbm,
    obuf,
    emb,
    gain,
    proj,
    ids,
    filt,
    res,
    rate,
    column,
    wproj,
    part,
    recv1,
    own,
    send2,
    recv2,
    en_all,
    tblkv,
    tblq,
    onehot,
    taps,
    weights,
    lquad,
    colw,
    step_rate,
    gated,
    qfilt,
    yintra,
    ends,
    carries,
    ybuf,
    load_sem,
    id_send,
    id_recv,
    s1_send,
    s1_recv,
    s2_send,
    s2_recv,
    e_send,
    e_recv,
    half_send,
    half_recv,
    here,
):
    seq = lax.axis_index("seq")
    tp = lax.axis_index("tp")
    core = lax.rem(tp, 2)
    far = tp // 2
    sibling = tp + 1 - 2 * core
    across_tp = lax.rem(tp + 2, 4)
    diagonal = lax.rem(sibling + 2, 4)
    peers_tp = (sibling, across_tp, diagonal)

    plane = 2 * max(seq_count // 16, 1)
    half = seq_count // 2

    def at(m):
        within = lax.rem(m, plane)
        return (within // 2) * 16 + (m // plane) * 2 + lax.rem(within, 2)

    def place_of(block):
        return lax.rem(block // 2, 8) * plane + (block // 16) * 2 + lax.rem(block, 2)

    me = place_of(seq)
    early = me < half
    known = jnp.where(early, half, seq_count)
    first_greeted = jnp.where(early, 0, half)
    partner = at(lax.rem(me + half, seq_count))

    def each_other(first, last, act):
        def one(m, _):
            @pl.when(m != me)
            def _():
                act(m)

            return 0

        lax.fori_loop(first, last, one, 0)

    barrier = pltpu.get_barrier_semaphore()

    def greet(m):
        pl.semaphore_signal(barrier, inc=1, device_id={"seq": at(m), "tp": tp}, device_id_type=MESH)

    each_other(first_greeted, seq_count, greet)
    for peer in peers_tp:
        pl.semaphore_signal(barrier, inc=1, device_id={"seq": seq, "tp": peer}, device_id_type=MESH)

    rows = emb_hbm.shape[0] // 4
    chan0 = pl.multiple_of(seq * LANES, LANES)
    loads = {}

    def load(name, slot, src, dst):
        loads[name] = pltpu.make_async_copy(src, dst, load_sem.at[slot])
        loads[name].start()

    load("gain", 1, gain_hbm, gain)
    for slot, name in enumerate(ORDER):
        load(f"proj{name}", 2 + slot, proj_hbm.at[name], proj.at[name])
    for r in range(4):
        load(f"emb{r}", 5 + r, emb_hbm.at[pl.ds(r * rows, rows), :], emb.at[pl.ds(r * rows, rows), :])
    load("ids", 0, ids_hbm, ids.at[me])
    load("rate", 9, rate_hbm.at[:, pl.ds(chan0, LANES)], rate)
    load("res", 10, res_hbm.at[:, pl.ds(chan0, LANES)], res)
    load("filt", 11, filt_hbm.at[:, :, pl.ds(chan0, LANES)], filt)

    def ids_to(m):
        return pltpu.make_async_remote_copy(
            src_ref=ids.at[me], dst_ref=ids.at[me],
            send_sem=id_send.at[m], recv_sem=id_recv.at[me],
            device_id={"seq": at(m), "tp": tp}, device_id_type=MESH,
        )

    def ids_from(m):
        return pltpu.make_async_remote_copy(
            src_ref=ids.at[m], dst_ref=ids.at[m],
            send_sem=id_send.at[m], recv_sem=id_recv.at[m],
            device_id={"seq": at(m), "tp": tp}, device_id_type=MESH,
        )

    def first_half():
        return pltpu.make_async_remote_copy(
            src_ref=ids.at[pl.ds(0, half)], dst_ref=ids.at[pl.ds(0, half)],
            send_sem=half_send, recv_sem=half_recv,
            device_id={"seq": partner, "tp": tp}, device_id_type=MESH,
        )

    def gained():
        features = proj.shape[1]
        loads["gain"].wait()
        gain_rows = gain.shape[0]
        turned = jnp.transpose(
            jnp.concatenate([gain[...], jnp.zeros((LANES - gain_rows, LANES), F32)], axis=0)
        )
        for k in range(gain_rows):
            column[k * LANES:(k + 1) * LANES, :] = jnp.broadcast_to(turned[:, k:k + 1], (LANES, LANES))
        for s in ORDER:
            loads[f"proj{s}"].wait()

            def one(k, _):
                span = pl.ds(pl.multiple_of(k * LANES, LANES), LANES)
                hi, lo = split(proj[s, span, :].astype(F32) * column[span, :])
                wproj[s, span, :] = jnp.concatenate([hi, lo], axis=1)
                return 0

            lax.fori_loop(0, features // LANES, one, 0, unroll=math.gcd(4, features // LANES))

    def project(s, first):
        for r in range(4):
            if first:
                loads[f"emb{r}"].wait()
            block = emb[pl.ds(r * rows, rows), :]
            both = jnp.dot(block, wproj[s], preferred_element_type=F32)
            turned = jnp.transpose(both[:, :LANES] + both[:, LANES:])
            for q in range(4):
                piece = turned[q * CHANNELS:(q + 1) * CHANNELS, :]
                part[s, q % 2, q // 2, :, r * rows:(r + 1) * rows] = piece

    def send_sibling(s):
        copy = pltpu.make_async_remote_copy(
            src_ref=part.at[s, 1 - core], dst_ref=recv1.at[s],
            send_sem=s1_send.at[s], recv_sem=s1_recv.at[s],
            device_id={"seq": seq, "tp": sibling}, device_id_type=MESH,
        )
        copy.start()
        return copy

    def send_across(s, copy):
        copy.wait_recv()
        send2[s] = part[s, core, 1 - far] + recv1[s, 1 - far]
        after = pltpu.make_async_remote_copy(
            src_ref=send2.at[s], dst_ref=recv2.at[s],
            send_sem=s2_send.at[s], recv_sem=s2_recv.at[s],
            device_id={"seq": seq, "tp": across_tp}, device_id_type=MESH,
        )
        after.start()
        own[s] = part[s, core, far] + recv1[s, far]
        return after

    def energies():
        for r in range(4):
            block = emb[pl.ds(r * rows, rows), :]
            total = jnp.zeros((rows, LANES), F32)
            for k in range(emb.shape[1] // LANES):
                piece = block[:, k * LANES:(k + 1) * LANES].astype(F32)
                total = total + piece * piece
            en_all[tp, pl.ds(r, 1), :] = jnp.sum(jnp.transpose(total), axis=0, keepdims=True)

    def energy_to(peer):
        return pltpu.make_async_remote_copy(
            src_ref=en_all.at[tp], dst_ref=en_all.at[tp], send_sem=e_send.at[peer], recv_sem=e_recv.at[tp],
            device_id={"seq": seq, "tp": peer}, device_id_type=MESH,
        )

    def energy_from(peer):
        return pltpu.make_async_remote_copy(
            src_ref=en_all.at[peer], dst_ref=en_all.at[peer], send_sem=e_send.at[peer], recv_sem=e_recv.at[peer],
            device_id={"seq": seq, "tp": peer}, device_id_type=MESH,
        )

    def enter():
        loads["ids"].wait()
        pl.semaphore_wait(barrier, known + 2)

        @pl.when(jnp.logical_not(early))
        def _():
            pl.semaphore_signal(here, inc=1, device_id={"seq": partner, "tp": tp}, device_id_type=MESH)

        each_other(0, known, lambda m: ids_to(m).start())

    def prepare():
        loads["rate"].wait()
        loads["res"].wait()
        loads["filt"].wait()
        turn = lax.rem(LANES - tp * CHANNELS, LANES)
        rates = pltpu.roll(rate[...], turn, 1)
        twice = 2.0 * rates
        series = twice * (
            1.0 - twice / 2 * (1.0 - twice / 3 * (1.0 - twice / 4 * (1.0 - twice / 5 * (1.0 - twice / 6))))
        )
        lost = jnp.where(twice < 0.125, series, 1.0 - jnp.exp(-twice))
        mode = pltpu.roll(res[...], turn, 1) * jnp.sqrt(lost)
        lane16 = lax.broadcasted_iota(jnp.int32, (MODES, LANES), 1).astype(F32)
        lquad[...] = jnp.zeros(lquad.shape, BF16)
        for c in range(CHANNELS):
            rate_c = jnp.broadcast_to(rates[:, c:c + 1], (MODES, LANES))
            mode_c = jnp.broadcast_to(mode[:, c:c + 1], (MODES, LANES))
            hi, lo = split(mode_c * jnp.exp(-rate_c * (lane16 + 1.0)))
            colw[pl.ds(c * MODES, MODES), :] = rate_c
            quad, at = c // 4, c % 4
            cols = pl.ds(at * LANES, LANES)
            lquad[quad, pl.ds(at * MODES, MODES), cols] = hi
            lquad[quad, pl.ds(64 + at * MODES, MODES), cols] = hi
            lquad[quad, pl.ds(128 + 64 * (quad % 2) + at * MODES, MODES), cols] = lo
        row_at = lax.broadcasted_iota(jnp.int32, (LANES, LANES), 0)
        lane_at = lax.broadcasted_iota(jnp.int32, (LANES, LANES), 1)
        behind = (LANES - 1 - row_at).astype(F32)
        keep = lane_at >= row_at

        def operators(g, _):
            start = pl.multiple_of(g * LANES, LANES)
            rate_row = jnp.transpose(colw[pl.ds(start, LANES), :])
            step_rate[g] = rate_row[:8, :] * LANES
            decays = jnp.exp(-rate_row * behind)
            e_hi, e_lo = split(decays)
            grown = quad_operands(jnp.exp(rate_row * (row_at + 1).astype(F32)))
            for half in range(2):
                kernels = jnp.dot(grown[half], lquad[g * 2 + half], preferred_element_type=F32)
                for at in range(4):
                    inner = jnp.where(keep, kernels[:, at * LANES:(at + 1) * LANES], 0.0)
                    t_hi, t_lo = split(inner)
                    c_in = half * 4 + at
                    mine = (lane_at >= c_in * MODES) & (lane_at < (c_in + 1) * MODES)
                    zero = jnp.zeros((LANES, LANES), F32)
                    m_hi = jnp.where(mine, e_hi.astype(F32), zero).astype(BF16)
                    m_lo = jnp.where(mine, e_lo.astype(F32), zero).astype(BF16)
                    c = g * 8 + c_in
                    weights[c, pl.ds(0, LANES), :] = jnp.concatenate([t_hi, m_hi], axis=1)
                    weights[c, pl.ds(LANES, LANES), :] = jnp.concatenate([t_lo, m_lo], axis=1)
            return 0

        lax.fori_loop(0, 4, operators, 0)

        for s in range(STREAMS):
            moved = pltpu.roll(filt[s], turn, 1)
            columns = jnp.transpose(jnp.concatenate([moved, jnp.zeros((LANES - TAPS, LANES), F32)], axis=0))
            for j in range(TAPS):
                taps[s * TAPS + j] = jnp.broadcast_to(columns[:CHANNELS, j:j + 1], (CHANNELS, LANES))

    gained()
    project(1, True)

    @pl.when(early)
    def _():
        project(2, False)
        project(0, False)

    enter()
    sib = {1: send_sibling(1)}

    @pl.when(jnp.logical_not(early))
    def _():
        project(2, False)

    sib[2] = send_sibling(2)
    cross = {1: send_across(1, sib[1])}

    @pl.when(jnp.logical_not(early))
    def _():
        project(0, False)

    sib[0] = send_sibling(0)
    cross[2] = send_across(2, sib[2])

    energies()
    for peer in peers_tp:
        energy_to(peer).start()
    cross[0] = send_across(0, sib[0])
    prepare()

    row_of = lax.broadcasted_iota(jnp.int32, (HALF, LANES), 0)

    def mark(m):
        low = jnp.broadcast_to(ids[m] & (HALF - 1), (HALF, LANES))
        onehot[at(m)] = jnp.where(row_of == low, 1.0, 0.0).astype(BF16)

    def arrive(m):
        ids_from(m).wait_recv()
        mark(m)

    mark(me)

    @pl.when(early)
    def _():
        each_other(0, half, arrive)
        pl.semaphore_wait(here, 1)
        first_half().start()

    for peer in peers_tp:
        energy_from(peer).wait_recv()
    scale = lax.rsqrt((en_all[0] + en_all[1] + en_all[2] + en_all[3]) / model_width + 1e-05)

    def tabulate(s, place, table):
        cross[s].wait_recv()
        height = table.shape[0] // 2
        for q in range(4):
            lanes = pl.ds(q * LANES, LANES)
            value = (own[s, :, lanes] + recv2[s, :, lanes]) * scale[q:q + 1, :]
            table[pl.ds((q // 2) * height + place * CHANNELS, CHANNELS), pl.ds((q % 2) * LANES, LANES)] = value.astype(BF16)

    tabulate(1, 0, tblkv)
    tabulate(2, 1, tblkv)
    each_other(half, seq_count, arrive)

    @pl.when(jnp.logical_not(early))
    def _():
        first_half().wait_recv()

        def one(m, _):
            mark(m)
            return 0

        lax.fori_loop(0, half, one, 0)

    def filter_streams(table, streams, unroll, emit):
        height = table.shape[0] // 2
        lane = lax.broadcasted_iota(jnp.int32, (height, LANES), 1)
        first_lane = lane < 1
        first_two = lane < 2

        def pair(i, carry):
            before1, before2 = carry
            hot = jnp.concatenate([onehot[2 * i], onehot[2 * i + 1]], axis=1)
            both = jnp.dot(table[...], hot, preferred_element_type=F32)
            for u in range(2):
                j = 2 * i + u
                upper = jnp.broadcast_to(ids[place_of(j)], (height, LANES)) >= HALF
                lanes = slice(u * LANES, (u + 1) * LANES)
                now = jnp.where(upper, both[height:, lanes], both[:height, lanes])
                one, two = pltpu.roll(now, 1, 1), pltpu.roll(now, 2, 1)
                back1 = jnp.where(first_lane, before1, one)
                back2 = jnp.where(first_two, before2, two)
                before1, before2 = one, two
                filtered = []
                for place, s in enumerate(streams):
                    mine = slice(place * CHANNELS, (place + 1) * CHANNELS)
                    filtered.append(
                        taps[s * TAPS] * now[mine] + taps[s * TAPS + 1] * back1[mine] + taps[s * TAPS + 2] * back2[mine]
                    )
                emit(pl.ds(pl.multiple_of(j * CHANNELS, CHANNELS), CHANNELS), *filtered)
            return before1, before2

        nothing = jnp.zeros((height, LANES), F32)
        lax.fori_loop(0, seq_count // 2, pair, (nothing, nothing), unroll=unroll)

    def emit_gated(at, k, v):
        gated[at, :] = (k * v).astype(BF16).astype(F32)

    def emit_query(at, q):
        qfilt[at, :] = q

    filter_streams(tblkv, (1, 2), 8, emit_gated)
    tabulate(0, 0, tblq)
    filter_streams(tblq, (0,), 8, emit_query)

    def inside(g, _):
        total = jnp.zeros((seq_count, LANES), F32)
        for at in range(8):
            c = g * 8 + at
            x = gated[pl.ds(c, seq_count, stride=CHANNELS), :].astype(BF16)
            result = jnp.dot(jnp.concatenate([x, x], axis=1), weights[c], preferred_element_type=F32)
            yintra[c] = result[:, :LANES]
            total = total + result[:, LANES:]
        ends[g] = total
        return 0

    lax.fori_loop(0, 4, inside, 0)

    sub = lax.broadcasted_iota(jnp.int32, (8, LANES), 0)
    for g in range(4):
        rate_row = step_rate[g]
        own_decay = jnp.exp(-rate_row * sub.astype(F32))
        eighth = jnp.exp(-rate_row * 8.0)
        factors = [(d, jnp.where(sub >= d, jnp.exp(-rate_row * float(d)), 0.0)) for d in (1, 2, 4)]
        entering = jnp.zeros((8, LANES), F32)
        for v in range(seq_count // 8):
            span = ends[g, pl.ds(v * 8, 8), :]
            for d, factor in factors:
                span = span + factor * pltpu.roll(span, d, 0)
            shifted = jnp.where(sub >= 1, pltpu.roll(span, 1, 0), 0.0)
            carries[g, pl.ds(v * 8, 8), :] = shifted + own_decay * entering
            entering = jnp.broadcast_to(span[7:8, :], (8, LANES)) + eighth * entering

    def across(g, _):
        operands = quad_operands(carries[g])
        for half in range(2):
            result = jnp.dot(operands[half], lquad[g * 2 + half], preferred_element_type=F32)
            for at in range(4):
                c = g * 8 + half * 4 + at
                ybuf[pl.ds(c, seq_count, stride=CHANNELS), :] = yintra[c] + result[:, at * LANES:(at + 1) * LANES]
        return 0

    lax.fori_loop(0, 4, across, 0)

    def gate(j, _):
        at = pl.ds(pl.multiple_of(j * CHANNELS, CHANNELS), CHANNELS)
        obuf[:, pl.ds(pl.multiple_of(j * LANES, LANES), LANES)] = (qfilt[at, :] * ybuf[at, :]).astype(BF16)
        return 0

    lax.fori_loop(0, seq_count, gate, 0, unroll=4)

    each_other(0, known, lambda m: ids_to(m).wait_send())
    pl.when(early)(first_half().wait_send)
    for copy in list(sib.values()) + list(cross.values()) + [energy_to(peer) for peer in peers_tp]:
        copy.wait_send()


def on_device(token_ids, embedding, norm_gain, projection, short_filter, residues, decay_rates):
    seq_count = lax.axis_size("seq")
    vocab, features = embedding.shape
    model_width = short_filter.shape[2]
    tokens = seq_count * LANES
    hbm = pl.BlockSpec(memory_space=pltpu.HBM)
    dma = pltpu.SemaphoreType.DMA
    vmem = pltpu.VMEM
    scratch = [
        vmem((vocab, features), BF16),
        vmem((features // LANES, LANES), F32),
        vmem((STREAMS, features, LANES), BF16),
        vmem((seq_count, 1, LANES), jnp.int32),
        vmem((STREAMS, TAPS, LANES), F32),
        vmem((MODES, LANES), F32),
        vmem((MODES, LANES), F32),
        vmem((features, LANES), F32),
        vmem((STREAMS, features, 2 * LANES), BF16),
        vmem((STREAMS, 2, 2, CHANNELS, vocab), F32),
        vmem((STREAMS, 2, CHANNELS, vocab), F32),
        vmem((STREAMS, CHANNELS, vocab), F32),
        vmem((STREAMS, CHANNELS, vocab), F32),
        vmem((STREAMS, CHANNELS, vocab), F32),
        vmem((4, 4, LANES), F32),
        vmem((4 * CHANNELS, HALF), BF16),
        vmem((2 * CHANNELS, HALF), BF16),
        vmem((seq_count, HALF, LANES), BF16),
        vmem((STREAMS * TAPS, CHANNELS, LANES), F32),
        vmem((CHANNELS, 2 * LANES, 2 * LANES), BF16),
        vmem((8, 2 * LANES, 4 * LANES), BF16),
        vmem((CHANNELS * MODES, LANES), F32),
        vmem((4, 8, LANES), F32),
        vmem((seq_count * CHANNELS, LANES), F32),
        vmem((seq_count * CHANNELS, LANES), F32),
        vmem((CHANNELS, seq_count, LANES), F32),
        vmem((4, seq_count, LANES), F32),
        vmem((4, seq_count, LANES), F32),
        vmem((seq_count * CHANNELS, LANES), F32),
        dma((12,)),
        dma((seq_count,)),
        dma((seq_count,)),
        dma((STREAMS,)),
        dma((STREAMS,)),
        dma((STREAMS,)),
        dma((STREAMS,)),
        dma((4,)),
        dma((4,)),
        dma(()),
        dma(()),
        pltpu.SemaphoreType.REGULAR,
    ]
    return pl.pallas_call(
        functools.partial(kernel, model_width, seq_count),
        out_shape=vmem((CHANNELS, tokens), BF16),
        in_specs=[hbm] * 7,
        out_specs=pl.BlockSpec(memory_space=vmem),
        scratch_shapes=scratch,
        compiler_params=pltpu.CompilerParams(
            collective_id=0, has_side_effects=True, vmem_limit_bytes=56 * 1024 * 1024
        ),
    )(
        embedding,
        norm_gain.reshape(features // LANES, LANES),
        jnp.transpose(projection, (1, 0, 2)),
        token_ids.reshape(1, LANES),
        short_filter,
        jnp.transpose(residues),
        jnp.transpose(decay_rates),
    )


def solution(mesh):
    return jax.shard_map(
        on_device,
        mesh=mesh,
        in_specs=(P("seq"), P(None, "tp"), P("tp"), P("tp", None, "seq"), P(), P(), P()),
        out_specs=P(("seq", "tp"), None),
        check_vma=False,
    )
```

```python
import functools
import math

import jax
import jax.numpy as jnp
from jax import lax
from jax.experimental import pallas as pl
from jax.experimental.pallas import tpu as pltpu
from jax.sharding import PartitionSpec as P

MESH = pl.DeviceIdType.MESH
F32 = jnp.float32
BF16 = jnp.bfloat16
LANES = 128
CHANNELS = 32
MODES = 16
STREAMS = 3
TAPS = 3
VOCAB = 512
HALF = 256
ORDER = (1, 2, 0)


def split(x):
    hi = x.astype(BF16)
    return hi, (x - hi.astype(F32)).astype(BF16)


def quad_operands(x):
    hi = x.astype(BF16).astype(F32)
    lo = x - hi
    lane = lax.broadcasted_iota(jnp.int32, x.shape, 1)
    low = lane < 64
    first = jnp.where(low, hi, pltpu.roll(lo, 64, 1))
    second = jnp.where(low, pltpu.roll(hi, 64, 1), lo)
    hi = hi.astype(BF16)
    return (
        jnp.concatenate([first.astype(BF16), hi], axis=1),
        jnp.concatenate([second.astype(BF16), hi], axis=1),
    )


def kernel(
    model_width,
    seq_count,
    emb_hbm,
    gain_hbm,
    proj_hbm,
    ids_hbm,
    filt_hbm,
    res_hbm,
    rate_hbm,
    obuf,
    emb,
    gain,
    proj,
    ids,
    filt,
    res,
    rate,
    column,
    wproj,
    part,
    recv1,
    own,
    send2,
    recv2,
    en_all,
    tblkv,
    tblq,
    onehot,
    taps,
    weights,
    lquad,
    colw,
    step_rate,
    gated,
    qfilt,
    yintra,
    ends,
    carries,
    ybuf,
    load_sem,
    id_send,
    id_recv,
    s1_send,
    s1_recv,
    s2_send,
    s2_recv,
    e_send,
    e_recv,
    piece_send,
    piece_recv,
    here,
):
    seq = lax.axis_index("seq")
    tp = lax.axis_index("tp")
    core = lax.rem(tp, 2)
    far = tp // 2
    sibling = tp + 1 - 2 * core
    across_tp = lax.rem(tp + 2, 4)
    diagonal = lax.rem(sibling + 2, 4)
    peers_tp = (sibling, across_tp, diagonal)

    plane = 2 * max(seq_count // 16, 1)
    half = seq_count // 2

    def at(m):
        within = lax.rem(m, plane)
        return (within // 2) * 16 + (m // plane) * 2 + lax.rem(within, 2)

    def place_of(block):
        return lax.rem(block // 2, 8) * plane + (block // 16) * 2 + lax.rem(block, 2)

    me = place_of(seq)
    quarter = seq_count // 4
    first = me < quarter
    early = me < half
    second = jnp.logical_and(early, jnp.logical_not(first))
    late = jnp.logical_not(early)
    known = jnp.where(first, quarter, jnp.where(early, half, seq_count))
    first_greeted = jnp.where(first, 0, jnp.where(early, quarter, half))
    near_partner = at(lax.rem(me + jnp.where(first, quarter, seq_count - quarter), seq_count))
    far_partner = at(lax.rem(me + half, seq_count))

    def each_other(first, last, act):
        def one(m, _):
            @pl.when(m != me)
            def _():
                act(m)

            return 0

        lax.fori_loop(first, last, one, 0)

    barrier = pltpu.get_barrier_semaphore()

    def greet(m):
        pl.semaphore_signal(barrier, inc=1, device_id={"seq": at(m), "tp": tp}, device_id_type=MESH)

    each_other(first_greeted, seq_count, greet)
    for peer in peers_tp:
        pl.semaphore_signal(barrier, inc=1, device_id={"seq": seq, "tp": peer}, device_id_type=MESH)

    rows = emb_hbm.shape[0] // 4
    chan0 = pl.multiple_of(seq * LANES, LANES)
    loads = {}

    def load(name, slot, src, dst):
        loads[name] = pltpu.make_async_copy(src, dst, load_sem.at[slot])
        loads[name].start()

    load("gain", 1, gain_hbm, gain)
    for slot, name in enumerate(ORDER):
        load(f"proj{name}", 2 + slot, proj_hbm.at[name], proj.at[name])
    for r in range(4):
        load(f"emb{r}", 5 + r, emb_hbm.at[pl.ds(r * rows, rows), :], emb.at[pl.ds(r * rows, rows), :])
    load("ids", 0, ids_hbm, ids.at[me])
    load("rate", 9, rate_hbm.at[:, pl.ds(chan0, LANES)], rate)
    load("res", 10, res_hbm.at[:, pl.ds(chan0, LANES)], res)
    load("filt", 11, filt_hbm.at[:, :, pl.ds(chan0, LANES)], filt)

    def ids_to(m):
        return pltpu.make_async_remote_copy(
            src_ref=ids.at[me], dst_ref=ids.at[me],
            send_sem=id_send.at[m], recv_sem=id_recv.at[me],
            device_id={"seq": at(m), "tp": tp}, device_id_type=MESH,
        )

    def ids_from(m):
        return pltpu.make_async_remote_copy(
            src_ref=ids.at[m], dst_ref=ids.at[m],
            send_sem=id_send.at[m], recv_sem=id_recv.at[m],
            device_id={"seq": at(m), "tp": tp}, device_id_type=MESH,
        )

    def in_one_piece(amount, slot, peer):
        return pltpu.make_async_remote_copy(
            src_ref=ids.at[pl.ds(0, amount)], dst_ref=ids.at[pl.ds(0, amount)],
            send_sem=piece_send.at[slot], recv_sem=piece_recv.at[slot],
            device_id={"seq": peer, "tp": tp}, device_id_type=MESH,
        )

    first_quarter = in_one_piece(quarter, 0, near_partner)
    first_half = in_one_piece(half, 1, far_partner)

    def gained():
        features = proj.shape[1]
        loads["gain"].wait()
        gain_rows = gain.shape[0]
        turned = jnp.transpose(
            jnp.concatenate([gain[...], jnp.zeros((LANES - gain_rows, LANES), F32)], axis=0)
        )
        for k in range(gain_rows):
            column[k * LANES:(k + 1) * LANES, :] = jnp.broadcast_to(turned[:, k:k + 1], (LANES, LANES))
        for s in ORDER:
            loads[f"proj{s}"].wait()

            def one(k, _):
                span = pl.ds(pl.multiple_of(k * LANES, LANES), LANES)
                hi, lo = split(proj[s, span, :].astype(F32) * column[span, :])
                wproj[s, span, :] = jnp.concatenate([hi, lo], axis=1)
                return 0

            lax.fori_loop(0, features // LANES, one, 0, unroll=math.gcd(4, features // LANES))

    def project(s, first):
        for r in range(4):
            if first:
                loads[f"emb{r}"].wait()
            block = emb[pl.ds(r * rows, rows), :]
            both = jnp.dot(block, wproj[s], preferred_element_type=F32)
            turned = jnp.transpose(both[:, :LANES] + both[:, LANES:])
            for q in range(4):
                piece = turned[q * CHANNELS:(q + 1) * CHANNELS, :]
                part[s, q % 2, q // 2, :, r * rows:(r + 1) * rows] = piece

    def send_sibling(s):
        copy = pltpu.make_async_remote_copy(
            src_ref=part.at[s, 1 - core], dst_ref=recv1.at[s],
            send_sem=s1_send.at[s], recv_sem=s1_recv.at[s],
            device_id={"seq": seq, "tp": sibling}, device_id_type=MESH,
        )
        copy.start()
        return copy

    def send_across(s, copy):
        copy.wait_recv()
        send2[s] = part[s, core, 1 - far] + recv1[s, 1 - far]
        after = pltpu.make_async_remote_copy(
            src_ref=send2.at[s], dst_ref=recv2.at[s],
            send_sem=s2_send.at[s], recv_sem=s2_recv.at[s],
            device_id={"seq": seq, "tp": across_tp}, device_id_type=MESH,
        )
        after.start()
        own[s] = part[s, core, far] + recv1[s, far]
        return after

    def energies():
        for r in range(4):
            block = emb[pl.ds(r * rows, rows), :]
            total = jnp.zeros((rows, LANES), F32)
            for k in range(emb.shape[1] // LANES):
                piece = block[:, k * LANES:(k + 1) * LANES].astype(F32)
                total = total + piece * piece
            en_all[tp, pl.ds(r, 1), :] = jnp.sum(jnp.transpose(total), axis=0, keepdims=True)

    def energy_to(peer):
        return pltpu.make_async_remote_copy(
            src_ref=en_all.at[tp], dst_ref=en_all.at[tp], send_sem=e_send.at[peer], recv_sem=e_recv.at[tp],
            device_id={"seq": seq, "tp": peer}, device_id_type=MESH,
        )

    def energy_from(peer):
        return pltpu.make_async_remote_copy(
            src_ref=en_all.at[peer], dst_ref=en_all.at[peer], send_sem=e_send.at[peer], recv_sem=e_recv.at[peer],
            device_id={"seq": seq, "tp": peer}, device_id_type=MESH,
        )

    def enter():
        loads["ids"].wait()
        pl.semaphore_wait(barrier, known + 2)

        @pl.when(second)
        def _():
            pl.semaphore_signal(here.at[0], inc=1, device_id={"seq": near_partner, "tp": tp}, device_id_type=MESH)

        @pl.when(late)
        def _():
            pl.semaphore_signal(here.at[1], inc=1, device_id={"seq": far_partner, "tp": tp}, device_id_type=MESH)

    def send_ids():
        each_other(0, known, lambda m: ids_to(m).start())

    def prepare():
        loads["rate"].wait()
        loads["res"].wait()
        loads["filt"].wait()
        turn = lax.rem(LANES - tp * CHANNELS, LANES)
        rates = pltpu.roll(rate[...], turn, 1)
        twice = 2.0 * rates
        series = twice * (
            1.0 - twice / 2 * (1.0 - twice / 3 * (1.0 - twice / 4 * (1.0 - twice / 5 * (1.0 - twice / 6))))
        )
        lost = jnp.where(twice < 0.125, series, 1.0 - jnp.exp(-twice))
        mode = pltpu.roll(res[...], turn, 1) * jnp.sqrt(lost)
        lane16 = lax.broadcasted_iota(jnp.int32, (MODES, LANES), 1).astype(F32)
        lquad[...] = jnp.zeros(lquad.shape, BF16)
        for c in range(CHANNELS):
            rate_c = jnp.broadcast_to(rates[:, c:c + 1], (MODES, LANES))
            mode_c = jnp.broadcast_to(mode[:, c:c + 1], (MODES, LANES))
            hi, lo = split(mode_c * jnp.exp(-rate_c * (lane16 + 1.0)))
            colw[pl.ds(c * MODES, MODES), :] = rate_c
            quad, at = c // 4, c % 4
            cols = pl.ds(at * LANES, LANES)
            lquad[quad, pl.ds(at * MODES, MODES), cols] = hi
            lquad[quad, pl.ds(64 + at * MODES, MODES), cols] = hi
            lquad[quad, pl.ds(128 + 64 * (quad % 2) + at * MODES, MODES), cols] = lo
        row_at = lax.broadcasted_iota(jnp.int32, (LANES, LANES), 0)
        lane_at = lax.broadcasted_iota(jnp.int32, (LANES, LANES), 1)
        behind = (LANES - 1 - row_at).astype(F32)
        keep = lane_at >= row_at

        def operators(g, _):
            start = pl.multiple_of(g * LANES, LANES)
            rate_row = jnp.transpose(colw[pl.ds(start, LANES), :])
            step_rate[g] = rate_row[:8, :] * LANES
            decays = jnp.exp(-rate_row * behind)
            e_hi, e_lo = split(decays)
            grown = quad_operands(jnp.exp(rate_row * (row_at + 1).astype(F32)))
            for half in range(2):
                kernels = jnp.dot(grown[half], lquad[g * 2 + half], preferred_element_type=F32)
                for at in range(4):
                    inner = jnp.where(keep, kernels[:, at * LANES:(at + 1) * LANES], 0.0)
                    t_hi, t_lo = split(inner)
                    c_in = half * 4 + at
                    mine = (lane_at >= c_in * MODES) & (lane_at < (c_in + 1) * MODES)
                    zero = jnp.zeros((LANES, LANES), F32)
                    m_hi = jnp.where(mine, e_hi.astype(F32), zero).astype(BF16)
                    m_lo = jnp.where(mine, e_lo.astype(F32), zero).astype(BF16)
                    c = g * 8 + c_in
                    weights[c, pl.ds(0, LANES), :] = jnp.concatenate([t_hi, m_hi], axis=1)
                    weights[c, pl.ds(LANES, LANES), :] = jnp.concatenate([t_lo, m_lo], axis=1)
            return 0

        lax.fori_loop(0, 4, operators, 0)

        for s in range(STREAMS):
            moved = pltpu.roll(filt[s], turn, 1)
            columns = jnp.transpose(jnp.concatenate([moved, jnp.zeros((LANES - TAPS, LANES), F32)], axis=0))
            for j in range(TAPS):
                taps[s * TAPS + j] = jnp.broadcast_to(columns[:CHANNELS, j:j + 1], (CHANNELS, LANES))

    gained()
    project(1, True)
    project(2, False)
    project(0, False)
    enter()
    sib = {s: send_sibling(s) for s in ORDER}
    send_ids()
    cross = {s: send_across(s, sib[s]) for s in ORDER}
    energies()
    for peer in peers_tp:
        energy_to(peer).start()
    prepare()

    row_of = lax.broadcasted_iota(jnp.int32, (HALF, LANES), 0)

    def mark(m):
        low = jnp.broadcast_to(ids[m] & (HALF - 1), (HALF, LANES))
        onehot[at(m)] = jnp.where(row_of == low, 1.0, 0.0).astype(BF16)

    def arrive(m):
        ids_from(m).wait_recv()
        mark(m)

    def mark_all(amount):
        def one(m, _):
            mark(m)
            return 0

        lax.fori_loop(0, amount, one, 0)

    mark(me)

    @pl.when(first)
    def _():
        each_other(0, quarter, arrive)
        pl.semaphore_wait(here.at[0], 1)
        first_quarter.start()

    @pl.when(early)
    def _():
        each_other(quarter, half, arrive)

    @pl.when(second)
    def _():
        first_quarter.wait_recv()
        mark_all(quarter)

    @pl.when(early)
    def _():
        pl.semaphore_wait(here.at[1], 1)
        first_half.start()

    for peer in peers_tp:
        energy_from(peer).wait_recv()
    scale = lax.rsqrt((en_all[0] + en_all[1] + en_all[2] + en_all[3]) / model_width + 1e-05)

    def tabulate(s, place, table):
        cross[s].wait_recv()
        height = table.shape[0] // 2
        for q in range(4):
            lanes = pl.ds(q * LANES, LANES)
            value = (own[s, :, lanes] + recv2[s, :, lanes]) * scale[q:q + 1, :]
            table[pl.ds((q // 2) * height + place * CHANNELS, CHANNELS), pl.ds((q % 2) * LANES, LANES)] = value.astype(BF16)

    tabulate(1, 0, tblkv)
    tabulate(2, 1, tblkv)
    each_other(half, seq_count, arrive)

    @pl.when(late)
    def _():
        first_half.wait_recv()
        mark_all(half)

    def filter_streams(table, streams, emit):
        height = table.shape[0] // 2
        lane = lax.broadcasted_iota(jnp.int32, (height, LANES), 1)
        first_lane = lane < 1
        first_two = lane < 2

        def pair(i, carry):
            before1, before2 = carry
            hot = jnp.concatenate([onehot[2 * i], onehot[2 * i + 1]], axis=1)
            both = jnp.dot(table[...], hot, preferred_element_type=F32)
            for u in range(2):
                j = 2 * i + u
                upper = jnp.broadcast_to(ids[place_of(j)], (height, LANES)) >= HALF
                lanes = slice(u * LANES, (u + 1) * LANES)
                now = jnp.where(upper, both[height:, lanes], both[:height, lanes])
                one, two = pltpu.roll(now, 1, 1), pltpu.roll(now, 2, 1)
                back1 = jnp.where(first_lane, before1, one)
                back2 = jnp.where(first_two, before2, two)
                before1, before2 = one, two
                filtered = []
                for place, s in enumerate(streams):
                    mine = slice(place * CHANNELS, (place + 1) * CHANNELS)
                    filtered.append(
                        taps[s * TAPS] * now[mine] + taps[s * TAPS + 1] * back1[mine] + taps[s * TAPS + 2] * back2[mine]
                    )
                emit(pl.ds(pl.multiple_of(j * CHANNELS, CHANNELS), CHANNELS), *filtered)
            return before1, before2

        nothing = jnp.zeros((height, LANES), F32)
        lax.fori_loop(0, seq_count // 2, pair, (nothing, nothing), unroll=seq_count // 2)

    def emit_gated(at, k, v):
        gated[at, :] = (k * v).astype(BF16).astype(F32)

    def emit_query(at, q):
        qfilt[at, :] = q

    filter_streams(tblkv, (1, 2), emit_gated)
    tabulate(0, 0, tblq)
    filter_streams(tblq, (0,), emit_query)

    def inside(g, _):
        total = jnp.zeros((seq_count, LANES), F32)
        for at in range(8):
            c = g * 8 + at
            x = gated[pl.ds(c, seq_count, stride=CHANNELS), :].astype(BF16)
            result = jnp.dot(jnp.concatenate([x, x], axis=1), weights[c], preferred_element_type=F32)
            yintra[c] = result[:, :LANES]
            total = total + result[:, LANES:]
        ends[g] = total
        return 0

    lax.fori_loop(0, 4, inside, 0, unroll=4)

    sub = lax.broadcasted_iota(jnp.int32, (8, LANES), 0)
    for g in range(4):
        rate_row = step_rate[g]
        own_decay = jnp.exp(-rate_row * sub.astype(F32))
        eighth = jnp.exp(-rate_row * 8.0)
        factors = [(d, jnp.where(sub >= d, jnp.exp(-rate_row * float(d)), 0.0)) for d in (1, 2, 4)]
        entering = jnp.zeros((8, LANES), F32)
        for v in range(seq_count // 8):
            span = ends[g, pl.ds(v * 8, 8), :]
            for d, factor in factors:
                span = span + factor * pltpu.roll(span, d, 0)
            shifted = jnp.where(sub >= 1, pltpu.roll(span, 1, 0), 0.0)
            carries[g, pl.ds(v * 8, 8), :] = shifted + own_decay * entering
            entering = jnp.broadcast_to(span[7:8, :], (8, LANES)) + eighth * entering

    def across(g, _):
        operands = quad_operands(carries[g])
        for half in range(2):
            result = jnp.dot(operands[half], lquad[g * 2 + half], preferred_element_type=F32)
            for at in range(4):
                c = g * 8 + half * 4 + at
                ybuf[pl.ds(c, seq_count, stride=CHANNELS), :] = yintra[c] + result[:, at * LANES:(at + 1) * LANES]
        return 0

    lax.fori_loop(0, 4, across, 0, unroll=4)

    def gate(j, _):
        at = pl.ds(pl.multiple_of(j * CHANNELS, CHANNELS), CHANNELS)
        obuf[:, pl.ds(pl.multiple_of(j * LANES, LANES), LANES)] = (qfilt[at, :] * ybuf[at, :]).astype(BF16)
        return 0

    lax.fori_loop(0, seq_count, gate, 0, unroll=8)

    each_other(0, known, lambda m: ids_to(m).wait_send())
    pl.when(first)(first_quarter.wait_send)
    pl.when(early)(first_half.wait_send)
    for copy in list(sib.values()) + list(cross.values()) + [energy_to(peer) for peer in peers_tp]:
        copy.wait_send()


def on_device(token_ids, embedding, norm_gain, projection, short_filter, residues, decay_rates):
    seq_count = lax.axis_size("seq")
    vocab, features = embedding.shape
    model_width = short_filter.shape[2]
    tokens = seq_count * LANES
    hbm = pl.BlockSpec(memory_space=pltpu.HBM)
    dma = pltpu.SemaphoreType.DMA
    vmem = pltpu.VMEM
    scratch = [
        vmem((vocab, features), BF16),
        vmem((features // LANES, LANES), F32),
        vmem((STREAMS, features, LANES), BF16),
        vmem((seq_count, 1, LANES), jnp.int32),
        vmem((STREAMS, TAPS, LANES), F32),
        vmem((MODES, LANES), F32),
        vmem((MODES, LANES), F32),
        vmem((features, LANES), F32),
        vmem((STREAMS, features, 2 * LANES), BF16),
        vmem((STREAMS, 2, 2, CHANNELS, vocab), F32),
        vmem((STREAMS, 2, CHANNELS, vocab), F32),
        vmem((STREAMS, CHANNELS, vocab), F32),
        vmem((STREAMS, CHANNELS, vocab), F32),
        vmem((STREAMS, CHANNELS, vocab), F32),
        vmem((4, 4, LANES), F32),
        vmem((4 * CHANNELS, HALF), BF16),
        vmem((2 * CHANNELS, HALF), BF16),
        vmem((seq_count, HALF, LANES), BF16),
        vmem((STREAMS * TAPS, CHANNELS, LANES), F32),
        vmem((CHANNELS, 2 * LANES, 2 * LANES), BF16),
        vmem((8, 2 * LANES, 4 * LANES), BF16),
        vmem((CHANNELS * MODES, LANES), F32),
        vmem((4, 8, LANES), F32),
        vmem((seq_count * CHANNELS, LANES), F32),
        vmem((seq_count * CHANNELS, LANES), F32),
        vmem((CHANNELS, seq_count, LANES), F32),
        vmem((4, seq_count, LANES), F32),
        vmem((4, seq_count, LANES), F32),
        vmem((seq_count * CHANNELS, LANES), F32),
        dma((12,)),
        dma((seq_count,)),
        dma((seq_count,)),
        dma((STREAMS,)),
        dma((STREAMS,)),
        dma((STREAMS,)),
        dma((STREAMS,)),
        dma((4,)),
        dma((4,)),
        dma((2,)),
        dma((2,)),
        pltpu.SemaphoreType.REGULAR((2,)),
    ]
    return pl.pallas_call(
        functools.partial(kernel, model_width, seq_count),
        out_shape=vmem((CHANNELS, tokens), BF16),
        in_specs=[hbm] * 7,
        out_specs=pl.BlockSpec(memory_space=vmem),
        scratch_shapes=scratch,
        compiler_params=pltpu.CompilerParams(
            collective_id=0, has_side_effects=True, vmem_limit_bytes=56 * 1024 * 1024
        ),
    )(
        embedding,
        norm_gain.reshape(features // LANES, LANES),
        jnp.transpose(projection, (1, 0, 2)),
        token_ids.reshape(1, LANES),
        short_filter,
        jnp.transpose(residues),
        jnp.transpose(decay_rates),
    )


def solution(mesh):
    return jax.shard_map(
        on_device,
        mesh=mesh,
        in_specs=(P("seq"), P(None, "tp"), P("tp"), P("tp", None, "seq"), P(), P(), P()),
        out_specs=P(("seq", "tp"), None),
        check_vma=False,
    )
```

```python
import functools
import math

import jax
import jax.numpy as jnp
from jax import lax
from jax.experimental import pallas as pl
from jax.experimental.pallas import tpu as pltpu
from jax.sharding import PartitionSpec as P

MESH = pl.DeviceIdType.MESH
F32 = jnp.float32
BF16 = jnp.bfloat16
LANES = 128
CHANNELS = 32
MODES = 16
STREAMS = 3
TAPS = 3
VOCAB = 512
HALF = 256
ORDER = (1, 2, 0)


def split(x):
    hi = x.astype(BF16)
    return hi, (x - hi.astype(F32)).astype(BF16)


def quad_operands(x):
    hi = x.astype(BF16).astype(F32)
    lo = x - hi
    lane = lax.broadcasted_iota(jnp.int32, x.shape, 1)
    low = lane < 64
    first = jnp.where(low, hi, pltpu.roll(lo, 64, 1))
    second = jnp.where(low, pltpu.roll(hi, 64, 1), lo)
    hi = hi.astype(BF16)
    return (
        jnp.concatenate([first.astype(BF16), hi], axis=1),
        jnp.concatenate([second.astype(BF16), hi], axis=1),
    )


def kernel(
    model_width,
    seq_count,
    emb_hbm,
    gain_hbm,
    proj_hbm,
    ids_hbm,
    filt_hbm,
    res_hbm,
    rate_hbm,
    obuf,
    emb,
    gain,
    proj,
    ids,
    filt,
    res,
    rate,
    column,
    wproj,
    part,
    recv1,
    own,
    send2,
    recv2,
    en_all,
    tblkv,
    tblq,
    onehot,
    taps,
    weights,
    lquad,
    colw,
    step_rate,
    gated,
    qfilt,
    yintra,
    ends,
    carries,
    ybuf,
    load_sem,
    id_send,
    id_recv,
    s1_send,
    s1_recv,
    s2_send,
    s2_recv,
    e_send,
    e_recv,
    piece_send,
    piece_recv,
    here,
):
    seq = lax.axis_index("seq")
    tp = lax.axis_index("tp")
    core = lax.rem(tp, 2)
    far = tp // 2
    sibling = tp + 1 - 2 * core
    across_tp = lax.rem(tp + 2, 4)
    diagonal = lax.rem(sibling + 2, 4)
    peers_tp = (sibling, across_tp, diagonal)

    plane = 2 * max(seq_count // 16, 1)
    half = seq_count // 2

    def at(m):
        within = lax.rem(m, plane)
        return (within // 2) * 16 + (m // plane) * 2 + lax.rem(within, 2)

    def place_of(block):
        return lax.rem(block // 2, 8) * plane + (block // 16) * 2 + lax.rem(block, 2)

    me = place_of(seq)
    quarter = seq_count // 4
    first = me < quarter
    early = me < half
    second = jnp.logical_and(early, jnp.logical_not(first))
    late = jnp.logical_not(early)
    known = jnp.where(first, quarter, jnp.where(early, half, seq_count))
    first_greeted = jnp.where(first, 0, jnp.where(early, quarter, half))
    group = me // quarter
    leader = at(lax.rem(me, quarter))

    def each_other(first, last, act):
        def one(m, _):
            @pl.when(m != me)
            def _():
                act(m)

            return 0

        lax.fori_loop(first, last, one, 0)

    rows = emb_hbm.shape[0] // 4
    chan0 = pl.multiple_of(seq * LANES, LANES)
    loads = {}

    def load(name, slot, src, dst):
        loads[name] = pltpu.make_async_copy(src, dst, load_sem.at[slot])
        loads[name].start()

    load("gain", 1, gain_hbm, gain)
    for slot, name in enumerate(ORDER):
        load(f"proj{name}", 2 + slot, proj_hbm.at[name], proj.at[name])
    for r in range(4):
        load(f"emb{r}", 5 + r, emb_hbm.at[pl.ds(r * rows, rows), :], emb.at[pl.ds(r * rows, rows), :])
    load("ids", 0, ids_hbm, ids.at[me])
    load("rate", 9, rate_hbm.at[:, pl.ds(chan0, LANES)], rate)
    load("res", 10, res_hbm.at[:, pl.ds(chan0, LANES)], res)
    load("filt", 11, filt_hbm.at[:, :, pl.ds(chan0, LANES)], filt)

    barrier = pltpu.get_barrier_semaphore()

    def greet(m):
        pl.semaphore_signal(barrier, inc=1, device_id={"seq": at(m), "tp": tp}, device_id_type=MESH)

    for peer in peers_tp:
        pl.semaphore_signal(barrier, inc=1, device_id={"seq": seq, "tp": peer}, device_id_type=MESH)
    each_other(first_greeted, seq_count, greet)

    def ids_to(m):
        return pltpu.make_async_remote_copy(
            src_ref=ids.at[me], dst_ref=ids.at[me],
            send_sem=id_send.at[m], recv_sem=id_recv.at[me],
            device_id={"seq": at(m), "tp": tp}, device_id_type=MESH,
        )

    def ids_from(m):
        return pltpu.make_async_remote_copy(
            src_ref=ids.at[m], dst_ref=ids.at[m],
            send_sem=id_send.at[m], recv_sem=id_recv.at[m],
            device_id={"seq": at(m), "tp": tp}, device_id_type=MESH,
        )

    def in_one_piece(amount, slot, peer):
        return pltpu.make_async_remote_copy(
            src_ref=ids.at[pl.ds(0, amount)], dst_ref=ids.at[pl.ds(0, amount)],
            send_sem=piece_send.at[slot], recv_sem=piece_recv.at[slot],
            device_id={"seq": peer, "tp": tp}, device_id_type=MESH,
        )

    def piece_to(later):
        return in_one_piece(quarter if later == 1 else half, later, at(lax.rem(me, quarter) + later * quarter))

    def gained():
        features = proj.shape[1]
        loads["gain"].wait()
        gain_rows = gain.shape[0]
        turned = jnp.transpose(
            jnp.concatenate([gain[...], jnp.zeros((LANES - gain_rows, LANES), F32)], axis=0)
        )
        for k in range(gain_rows):
            column[k * LANES:(k + 1) * LANES, :] = jnp.broadcast_to(turned[:, k:k + 1], (LANES, LANES))
        for s in ORDER:
            loads[f"proj{s}"].wait()

            def one(k, _):
                span = pl.ds(pl.multiple_of(k * LANES, LANES), LANES)
                hi, lo = split(proj[s, span, :].astype(F32) * column[span, :])
                wproj[s, span, :] = jnp.concatenate([hi, lo], axis=1)
                return 0

            lax.fori_loop(0, features // LANES, one, 0, unroll=math.gcd(4, features // LANES))

    def project(s, first):
        for r in range(4):
            if first:
                loads[f"emb{r}"].wait()
            block = emb[pl.ds(r * rows, rows), :]
            both = jnp.dot(block, wproj[s], preferred_element_type=F32)
            turned = jnp.transpose(both[:, :LANES] + both[:, LANES:])
            for q in range(4):
                piece = turned[q * CHANNELS:(q + 1) * CHANNELS, :]
                part[s, q % 2, q // 2, :, r * rows:(r + 1) * rows] = piece

    def send_sibling(s):
        copy = pltpu.make_async_remote_copy(
            src_ref=part.at[s, 1 - core], dst_ref=recv1.at[s],
            send_sem=s1_send.at[s], recv_sem=s1_recv.at[s],
            device_id={"seq": seq, "tp": sibling}, device_id_type=MESH,
        )
        copy.start()
        return copy

    def send_across(s, copy):
        copy.wait_recv()
        send2[s] = part[s, core, 1 - far] + recv1[s, 1 - far]
        after = pltpu.make_async_remote_copy(
            src_ref=send2.at[s], dst_ref=recv2.at[s],
            send_sem=s2_send.at[s], recv_sem=s2_recv.at[s],
            device_id={"seq": seq, "tp": across_tp}, device_id_type=MESH,
        )
        after.start()
        own[s] = part[s, core, far] + recv1[s, far]
        return after

    def energies():
        for r in range(4):
            block = emb[pl.ds(r * rows, rows), :]
            total = jnp.zeros((rows, LANES), F32)
            for k in range(emb.shape[1] // LANES):
                piece = block[:, k * LANES:(k + 1) * LANES].astype(F32)
                total = total + piece * piece
            en_all[tp, pl.ds(r, 1), :] = jnp.sum(jnp.transpose(total), axis=0, keepdims=True)

    def energy_to(peer):
        return pltpu.make_async_remote_copy(
            src_ref=en_all.at[tp], dst_ref=en_all.at[tp], send_sem=e_send.at[peer], recv_sem=e_recv.at[tp],
            device_id={"seq": seq, "tp": peer}, device_id_type=MESH,
        )

    def energy_from(peer):
        return pltpu.make_async_remote_copy(
            src_ref=en_all.at[peer], dst_ref=en_all.at[peer], send_sem=e_send.at[peer], recv_sem=e_recv.at[peer],
            device_id={"seq": seq, "tp": peer}, device_id_type=MESH,
        )

    def enter():
        loads["ids"].wait()
        pl.semaphore_wait(barrier, known + 2)

        @pl.when(jnp.logical_not(first))
        def _():
            pl.semaphore_signal(here.at[group], inc=1, device_id={"seq": leader, "tp": tp}, device_id_type=MESH)

    def send_ids():
        each_other(0, known, lambda m: ids_to(m).start())

    def prepare():
        loads["rate"].wait()
        loads["res"].wait()
        loads["filt"].wait()
        turn = lax.rem(LANES - tp * CHANNELS, LANES)
        rates = pltpu.roll(rate[...], turn, 1)
        twice = 2.0 * rates
        series = twice * (
            1.0 - twice / 2 * (1.0 - twice / 3 * (1.0 - twice / 4 * (1.0 - twice / 5 * (1.0 - twice / 6))))
        )
        lost = jnp.where(twice < 0.125, series, 1.0 - jnp.exp(-twice))
        mode = pltpu.roll(res[...], turn, 1) * jnp.sqrt(lost)
        lane16 = lax.broadcasted_iota(jnp.int32, (MODES, LANES), 1).astype(F32)
        lquad[...] = jnp.zeros(lquad.shape, BF16)
        for c in range(CHANNELS):
            rate_c = jnp.broadcast_to(rates[:, c:c + 1], (MODES, LANES))
            mode_c = jnp.broadcast_to(mode[:, c:c + 1], (MODES, LANES))
            hi, lo = split(mode_c * jnp.exp(-rate_c * (lane16 + 1.0)))
            colw[pl.ds(c * MODES, MODES), :] = rate_c
            quad, at = c // 4, c % 4
            cols = pl.ds(at * LANES, LANES)
            lquad[quad, pl.ds(at * MODES, MODES), cols] = hi
            lquad[quad, pl.ds(64 + at * MODES, MODES), cols] = hi
            lquad[quad, pl.ds(128 + 64 * (quad % 2) + at * MODES, MODES), cols] = lo
        row_at = lax.broadcasted_iota(jnp.int32, (LANES, LANES), 0)
        lane_at = lax.broadcasted_iota(jnp.int32, (LANES, LANES), 1)
        behind = (LANES - 1 - row_at).astype(F32)
        keep = lane_at >= row_at

        def operators(g, _):
            start = pl.multiple_of(g * LANES, LANES)
            rate_row = jnp.transpose(colw[pl.ds(start, LANES), :])
            step_rate[g] = rate_row[:8, :] * LANES
            decays = jnp.exp(-rate_row * behind)
            e_hi, e_lo = split(decays)
            grown = quad_operands(jnp.exp(rate_row * (row_at + 1).astype(F32)))
            for half in range(2):
                kernels = jnp.dot(grown[half], lquad[g * 2 + half], preferred_element_type=F32)
                for at in range(4):
                    inner = jnp.where(keep, kernels[:, at * LANES:(at + 1) * LANES], 0.0)
                    t_hi, t_lo = split(inner)
                    c_in = half * 4 + at
                    mine = (lane_at >= c_in * MODES) & (lane_at < (c_in + 1) * MODES)
                    zero = jnp.zeros((LANES, LANES), F32)
                    m_hi = jnp.where(mine, e_hi.astype(F32), zero).astype(BF16)
                    m_lo = jnp.where(mine, e_lo.astype(F32), zero).astype(BF16)
                    c = g * 8 + c_in
                    weights[c, pl.ds(0, LANES), :] = jnp.concatenate([t_hi, m_hi], axis=1)
                    weights[c, pl.ds(LANES, LANES), :] = jnp.concatenate([t_lo, m_lo], axis=1)
            return 0

        lax.fori_loop(0, 4, operators, 0)

        for s in range(STREAMS):
            moved = pltpu.roll(filt[s], turn, 1)
            columns = jnp.transpose(jnp.concatenate([moved, jnp.zeros((LANES - TAPS, LANES), F32)], axis=0))
            for j in range(TAPS):
                taps[s * TAPS + j] = jnp.broadcast_to(columns[:CHANNELS, j:j + 1], (CHANNELS, LANES))

    gained()
    project(1, True)
    project(2, False)
    project(0, False)
    enter()
    sib = {s: send_sibling(s) for s in ORDER}
    send_ids()
    cross = {s: send_across(s, sib[s]) for s in ORDER}
    energies()
    for peer in peers_tp:
        energy_to(peer).start()
    prepare()
    each_other(0, known, lambda m: ids_to(m).wait_send())
    for copy in list(sib.values()) + [energy_to(peer) for peer in peers_tp]:
        copy.wait_send()

    row_of = lax.broadcasted_iota(jnp.int32, (HALF, LANES), 0)

    def mark(m):
        low = jnp.broadcast_to(ids[m] & (HALF - 1), (HALF, LANES))
        onehot[at(m)] = jnp.where(row_of == low, 1.0, 0.0).astype(BF16)

    def arrive(m):
        ids_from(m).wait_recv()
        mark(m)

    def mark_all(amount):
        def one(m, _):
            mark(m)
            return 0

        lax.fori_loop(0, amount, one, 0)

    mark(me)

    @pl.when(first)
    def _():
        each_other(0, quarter, arrive)
        pl.semaphore_wait(here.at[1], 1)
        piece_to(1).start()

    @pl.when(early)
    def _():
        each_other(quarter, half, arrive)

    @pl.when(first)
    def _():
        for later in (2, 3):
            pl.semaphore_wait(here.at[later], 1)
            piece_to(later).start()

    @pl.when(second)
    def _():
        in_one_piece(quarter, 1, leader).wait_recv()
        mark_all(quarter)

    for peer in peers_tp:
        energy_from(peer).wait_recv()
    scale = lax.rsqrt((en_all[0] + en_all[1] + en_all[2] + en_all[3]) / model_width + 1e-05)

    def tabulate(s, place, table):
        cross[s].wait_recv()
        height = table.shape[0] // 2
        for q in range(4):
            lanes = pl.ds(q * LANES, LANES)
            value = (own[s, :, lanes] + recv2[s, :, lanes]) * scale[q:q + 1, :]
            table[pl.ds((q // 2) * height + place * CHANNELS, CHANNELS), pl.ds((q % 2) * LANES, LANES)] = value.astype(BF16)

    tabulate(1, 0, tblkv)
    tabulate(2, 1, tblkv)
    each_other(half, seq_count, arrive)

    @pl.when(late)
    def _():
        in_one_piece(half, group, leader).wait_recv()
        mark_all(half)

    def filter_streams(table, streams, emit):
        height = table.shape[0] // 2
        lane = lax.broadcasted_iota(jnp.int32, (height, LANES), 1)
        first_lane = lane < 1
        first_two = lane < 2

        def pair(i, carry):
            before1, before2 = carry
            hot = jnp.concatenate([onehot[2 * i], onehot[2 * i + 1]], axis=1)
            both = jnp.dot(table[...], hot, preferred_element_type=F32)
            for u in range(2):
                j = 2 * i + u
                upper = jnp.broadcast_to(ids[place_of(j)], (height, LANES)) >= HALF
                lanes = slice(u * LANES, (u + 1) * LANES)
                now = jnp.where(upper, both[height:, lanes], both[:height, lanes])
                one, two = pltpu.roll(now, 1, 1), pltpu.roll(now, 2, 1)
                back1 = jnp.where(first_lane, before1, one)
                back2 = jnp.where(first_two, before2, two)
                before1, before2 = one, two
                filtered = []
                for place, s in enumerate(streams):
                    mine = slice(place * CHANNELS, (place + 1) * CHANNELS)
                    filtered.append(
                        taps[s * TAPS] * now[mine] + taps[s * TAPS + 1] * back1[mine] + taps[s * TAPS + 2] * back2[mine]
                    )
                emit(pl.ds(pl.multiple_of(j * CHANNELS, CHANNELS), CHANNELS), *filtered)
            return before1, before2

        nothing = jnp.zeros((height, LANES), F32)
        lax.fori_loop(0, seq_count // 2, pair, (nothing, nothing), unroll=seq_count // 2)

    def emit_gated(at, k, v):
        gated[at, :] = (k * v).astype(BF16).astype(F32)

    def emit_query(at, q):
        qfilt[at, :] = q

    filter_streams(tblkv, (1, 2), emit_gated)
    tabulate(0, 0, tblq)
    filter_streams(tblq, (0,), emit_query)

    def inside(g, _):
        total = jnp.zeros((seq_count, LANES), F32)
        for at in range(8):
            c = g * 8 + at
            x = gated[pl.ds(c, seq_count, stride=CHANNELS), :].astype(BF16)
            result = jnp.dot(jnp.concatenate([x, x], axis=1), weights[c], preferred_element_type=F32)
            yintra[c] = result[:, :LANES]
            total = total + result[:, LANES:]
        ends[g] = total
        return 0

    lax.fori_loop(0, 4, inside, 0, unroll=4)

    sub = lax.broadcasted_iota(jnp.int32, (8, LANES), 0)
    for g in range(4):
        rate_row = step_rate[g]
        own_decay = jnp.exp(-rate_row * sub.astype(F32))
        eighth = jnp.exp(-rate_row * 8.0)
        factors = [(d, jnp.where(sub >= d, jnp.exp(-rate_row * float(d)), 0.0)) for d in (1, 2, 4)]
        entering = jnp.zeros((8, LANES), F32)
        for v in range(seq_count // 8):
            span = ends[g, pl.ds(v * 8, 8), :]
            for d, factor in factors:
                span = span + factor * pltpu.roll(span, d, 0)
            shifted = jnp.where(sub >= 1, pltpu.roll(span, 1, 0), 0.0)
            carries[g, pl.ds(v * 8, 8), :] = shifted + own_decay * entering
            entering = jnp.broadcast_to(span[7:8, :], (8, LANES)) + eighth * entering

    def across(g, _):
        operands = quad_operands(carries[g])
        for half in range(2):
            result = jnp.dot(operands[half], lquad[g * 2 + half], preferred_element_type=F32)
            for at in range(4):
                c = g * 8 + half * 4 + at
                ybuf[pl.ds(c, seq_count, stride=CHANNELS), :] = yintra[c] + result[:, at * LANES:(at + 1) * LANES]
        return 0

    lax.fori_loop(0, 4, across, 0, unroll=4)

    def gate(j, _):
        at = pl.ds(pl.multiple_of(j * CHANNELS, CHANNELS), CHANNELS)
        obuf[:, pl.ds(pl.multiple_of(j * LANES, LANES), LANES)] = (qfilt[at, :] * ybuf[at, :]).astype(BF16)
        return 0

    lax.fori_loop(0, seq_count, gate, 0, unroll=8)


    @pl.when(first)
    def _():
        for later in (1, 2, 3):
            piece_to(later).wait_send()

    for copy in cross.values():
        copy.wait_send()


def on_device(token_ids, embedding, norm_gain, projection, short_filter, residues, decay_rates):
    seq_count = lax.axis_size("seq")
    vocab, features = embedding.shape
    model_width = short_filter.shape[2]
    tokens = seq_count * LANES
    hbm = pl.BlockSpec(memory_space=pltpu.HBM)
    dma = pltpu.SemaphoreType.DMA
    vmem = pltpu.VMEM
    scratch = [
        vmem((vocab, features), BF16),
        vmem((features // LANES, LANES), F32),
        vmem((STREAMS, features, LANES), BF16),
        vmem((seq_count, 1, LANES), jnp.int32),
        vmem((STREAMS, TAPS, LANES), F32),
        vmem((MODES, LANES), F32),
        vmem((MODES, LANES), F32),
        vmem((features, LANES), F32),
        vmem((STREAMS, features, 2 * LANES), BF16),
        vmem((STREAMS, 2, 2, CHANNELS, vocab), F32),
        vmem((STREAMS, 2, CHANNELS, vocab), F32),
        vmem((STREAMS, CHANNELS, vocab), F32),
        vmem((STREAMS, CHANNELS, vocab), F32),
        vmem((STREAMS, CHANNELS, vocab), F32),
        vmem((4, 4, LANES), F32),
        vmem((4 * CHANNELS, HALF), BF16),
        vmem((2 * CHANNELS, HALF), BF16),
        vmem((seq_count, HALF, LANES), BF16),
        vmem((STREAMS * TAPS, CHANNELS, LANES), F32),
        vmem((CHANNELS, 2 * LANES, 2 * LANES), BF16),
        vmem((8, 2 * LANES, 4 * LANES), BF16),
        vmem((CHANNELS * MODES, LANES), F32),
        vmem((4, 8, LANES), F32),
        vmem((seq_count * CHANNELS, LANES), F32),
        vmem((seq_count * CHANNELS, LANES), F32),
        vmem((CHANNELS, seq_count, LANES), F32),
        vmem((4, seq_count, LANES), F32),
        vmem((4, seq_count, LANES), F32),
        vmem((seq_count * CHANNELS, LANES), F32),
        dma((12,)),
        dma((seq_count,)),
        dma((seq_count,)),
        dma((STREAMS,)),
        dma((STREAMS,)),
        dma((STREAMS,)),
        dma((STREAMS,)),
        dma((4,)),
        dma((4,)),
        dma((4,)),
        dma((4,)),
        pltpu.SemaphoreType.REGULAR((4,)),
    ]
    return pl.pallas_call(
        functools.partial(kernel, model_width, seq_count),
        out_shape=vmem((CHANNELS, tokens), BF16),
        in_specs=[hbm] * 7,
        out_specs=pl.BlockSpec(memory_space=vmem),
        scratch_shapes=scratch,
        compiler_params=pltpu.CompilerParams(
            collective_id=0, has_side_effects=True, vmem_limit_bytes=56 * 1024 * 1024
        ),
    )(
        embedding,
        norm_gain.reshape(features // LANES, LANES),
        jnp.transpose(projection, (1, 0, 2)),
        token_ids.reshape(1, LANES),
        short_filter,
        jnp.transpose(residues),
        jnp.transpose(decay_rates),
    )


def solution(mesh):
    return jax.shard_map(
        on_device,
        mesh=mesh,
        in_specs=(P("seq"), P(None, "tp"), P("tp"), P("tp", None, "seq"), P(), P(), P()),
        out_specs=P(("seq", "tp"), None),
        check_vma=False,
    )
```

```python
import functools
import math

import jax
import jax.numpy as jnp
from jax import lax
from jax.experimental import pallas as pl
from jax.experimental.pallas import tpu as pltpu
from jax.sharding import PartitionSpec as P

MESH = pl.DeviceIdType.MESH
F32 = jnp.float32
BF16 = jnp.bfloat16
LANES = 128
CHANNELS = 32
MODES = 16
STREAMS = 3
TAPS = 3
VOCAB = 512
HALF = 256
ORDER = (1, 2, 0)


def split(x):
    hi = x.astype(BF16)
    return hi, (x - hi.astype(F32)).astype(BF16)


def quad_operands(x):
    hi = x.astype(BF16).astype(F32)
    lo = x - hi
    lane = lax.broadcasted_iota(jnp.int32, x.shape, 1)
    low = lane < 64
    first = jnp.where(low, hi, pltpu.roll(lo, 64, 1))
    second = jnp.where(low, pltpu.roll(hi, 64, 1), lo)
    hi = hi.astype(BF16)
    return (
        jnp.concatenate([first.astype(BF16), hi], axis=1),
        jnp.concatenate([second.astype(BF16), hi], axis=1),
    )


def kernel(
    model_width,
    seq_count,
    emb_hbm,
    gain_hbm,
    proj_hbm,
    ids_hbm,
    filt_hbm,
    res_hbm,
    rate_hbm,
    obuf,
    emb,
    gain,
    proj,
    ids,
    filt,
    res,
    rate,
    column,
    wproj,
    part,
    recv1,
    own,
    send2,
    recv2,
    en_all,
    tblkv,
    tblq,
    onehot,
    taps,
    weights,
    lquad,
    colw,
    step_rate,
    gated,
    qfilt,
    yintra,
    ends,
    carries,
    ybuf,
    load_sem,
    id_send,
    id_recv,
    s1_send,
    s1_recv,
    s2_send,
    s2_recv,
    e_send,
    e_recv,
    piece_send,
    piece_recv,
    here,
):
    seq = lax.axis_index("seq")
    tp = lax.axis_index("tp")
    core = lax.rem(tp, 2)
    far = tp // 2
    sibling = tp + 1 - 2 * core
    across_tp = lax.rem(tp + 2, 4)
    diagonal = lax.rem(sibling + 2, 4)
    peers_tp = (sibling, across_tp, diagonal)

    plane = 2 * max(seq_count // 16, 1)
    half = seq_count // 2

    def at(m):
        within = lax.rem(m, plane)
        return (within // 2) * 16 + (m // plane) * 2 + lax.rem(within, 2)

    def place_of(block):
        return lax.rem(block // 2, 8) * plane + (block // 16) * 2 + lax.rem(block, 2)

    me = place_of(seq)
    quarter = seq_count // 4
    first = me < quarter
    early = me < half
    second = jnp.logical_and(early, jnp.logical_not(first))
    late = jnp.logical_not(early)
    known = jnp.where(first, quarter, jnp.where(early, half, seq_count))
    first_greeted = jnp.where(first, 0, jnp.where(early, quarter, half))
    group = me // quarter
    leader = at(lax.rem(me, quarter))

    def each_other(first, last, act):
        def one(m, _):
            @pl.when(m != me)
            def _():
                act(m)

            return 0

        lax.fori_loop(first, last, one, 0)

    rows = emb_hbm.shape[0] // 4
    chan0 = pl.multiple_of(seq * LANES, LANES)
    loads = {}

    def load(name, slot, src, dst):
        loads[name] = pltpu.make_async_copy(src, dst, load_sem.at[slot])
        loads[name].start()

    load("gain", 1, gain_hbm, gain)
    for slot, name in enumerate(ORDER):
        load(f"proj{name}", 2 + slot, proj_hbm.at[name], proj.at[name])
    for r in range(4):
        load(f"emb{r}", 5 + r, emb_hbm.at[pl.ds(r * rows, rows), :], emb.at[pl.ds(r * rows, rows), :])
    load("ids", 0, ids_hbm, ids.at[me])
    load("rate", 9, rate_hbm.at[:, pl.ds(chan0, LANES)], rate)
    load("res", 10, res_hbm.at[:, pl.ds(chan0, LANES)], res)
    load("filt", 11, filt_hbm.at[:, :, pl.ds(chan0, LANES)], filt)

    barrier = pltpu.get_barrier_semaphore()

    def greet(m):
        pl.semaphore_signal(barrier, inc=1, device_id={"seq": at(m), "tp": tp}, device_id_type=MESH)

    for peer in peers_tp:
        pl.semaphore_signal(barrier, inc=1, device_id={"seq": seq, "tp": peer}, device_id_type=MESH)
    each_other(first_greeted, seq_count, greet)

    def ids_to(m):
        return pltpu.make_async_remote_copy(
            src_ref=ids.at[me], dst_ref=ids.at[me],
            send_sem=id_send.at[m], recv_sem=id_recv.at[me],
            device_id={"seq": at(m), "tp": tp}, device_id_type=MESH,
        )

    def ids_from(m):
        return pltpu.make_async_remote_copy(
            src_ref=ids.at[m], dst_ref=ids.at[m],
            send_sem=id_send.at[m], recv_sem=id_recv.at[m],
            device_id={"seq": at(m), "tp": tp}, device_id_type=MESH,
        )

    def in_one_piece(amount, slot, peer):
        return pltpu.make_async_remote_copy(
            src_ref=ids.at[pl.ds(0, amount)], dst_ref=ids.at[pl.ds(0, amount)],
            send_sem=piece_send.at[slot], recv_sem=piece_recv.at[slot],
            device_id={"seq": peer, "tp": tp}, device_id_type=MESH,
        )

    def piece_to(later):
        return in_one_piece(quarter if later == 1 else half, later, at(lax.rem(me, quarter) + later * quarter))

    def gained():
        features = proj.shape[1]
        loads["gain"].wait()
        gain_rows = gain.shape[0]
        turned = jnp.transpose(
            jnp.concatenate([gain[...], jnp.zeros((LANES - gain_rows, LANES), F32)], axis=0)
        )
        for k in range(gain_rows):
            column[k * LANES:(k + 1) * LANES, :] = jnp.broadcast_to(turned[:, k:k + 1], (LANES, LANES))
        for s in ORDER:
            loads[f"proj{s}"].wait()

            def one(k, _):
                span = pl.ds(pl.multiple_of(k * LANES, LANES), LANES)
                hi, lo = split(proj[s, span, :].astype(F32) * column[span, :])
                wproj[s, span, :] = jnp.concatenate([hi, lo], axis=1)
                return 0

            lax.fori_loop(0, features // LANES, one, 0, unroll=math.gcd(4, features // LANES))

    def project(s, first):
        for r in range(4):
            if first:
                loads[f"emb{r}"].wait()
            block = emb[pl.ds(r * rows, rows), :]
            both = jnp.dot(block, wproj[s], preferred_element_type=F32)
            turned = jnp.transpose(both[:, :LANES] + both[:, LANES:])
            for q in range(4):
                piece = turned[q * CHANNELS:(q + 1) * CHANNELS, :]
                part[s, q % 2, q // 2, :, r * rows:(r + 1) * rows] = piece

    def send_sibling(s):
        copy = pltpu.make_async_remote_copy(
            src_ref=part.at[s, 1 - core], dst_ref=recv1.at[s],
            send_sem=s1_send.at[s], recv_sem=s1_recv.at[s],
            device_id={"seq": seq, "tp": sibling}, device_id_type=MESH,
        )
        copy.start()
        return copy

    def send_across(s, copy):
        copy.wait_recv()
        send2[s] = part[s, core, 1 - far] + recv1[s, 1 - far]
        after = pltpu.make_async_remote_copy(
            src_ref=send2.at[s], dst_ref=recv2.at[s],
            send_sem=s2_send.at[s], recv_sem=s2_recv.at[s],
            device_id={"seq": seq, "tp": across_tp}, device_id_type=MESH,
        )
        after.start()
        own[s] = part[s, core, far] + recv1[s, far]
        return after

    def energies():
        for r in range(4):
            block = emb[pl.ds(r * rows, rows), :]
            total = jnp.zeros((rows, LANES), F32)
            for k in range(emb.shape[1] // LANES):
                piece = block[:, k * LANES:(k + 1) * LANES].astype(F32)
                total = total + piece * piece
            en_all[tp, pl.ds(r, 1), :] = jnp.sum(jnp.transpose(total), axis=0, keepdims=True)

    def energy_to(peer):
        return pltpu.make_async_remote_copy(
            src_ref=en_all.at[tp], dst_ref=en_all.at[tp], send_sem=e_send.at[peer], recv_sem=e_recv.at[tp],
            device_id={"seq": seq, "tp": peer}, device_id_type=MESH,
        )

    def energy_from(peer):
        return pltpu.make_async_remote_copy(
            src_ref=en_all.at[peer], dst_ref=en_all.at[peer], send_sem=e_send.at[peer], recv_sem=e_recv.at[peer],
            device_id={"seq": seq, "tp": peer}, device_id_type=MESH,
        )

    def enter():
        loads["ids"].wait()
        pl.semaphore_wait(barrier, known + 2)

        @pl.when(jnp.logical_not(first))
        def _():
            pl.semaphore_signal(here.at[group], inc=1, device_id={"seq": leader, "tp": tp}, device_id_type=MESH)

    def send_ids():
        each_other(0, known, lambda m: ids_to(m).start())

    def prepare():
        loads["rate"].wait()
        loads["res"].wait()
        loads["filt"].wait()
        turn = lax.rem(LANES - tp * CHANNELS, LANES)
        rates = pltpu.roll(rate[...], turn, 1)
        twice = 2.0 * rates
        series = twice * (
            1.0 - twice / 2 * (1.0 - twice / 3 * (1.0 - twice / 4 * (1.0 - twice / 5 * (1.0 - twice / 6))))
        )
        lost = jnp.where(twice < 0.125, series, 1.0 - jnp.exp(-twice))
        mode = pltpu.roll(res[...], turn, 1) * jnp.sqrt(lost)
        lane16 = lax.broadcasted_iota(jnp.int32, (MODES, LANES), 1).astype(F32)
        lquad[...] = jnp.zeros(lquad.shape, BF16)
        for c in range(CHANNELS):
            rate_c = jnp.broadcast_to(rates[:, c:c + 1], (MODES, LANES))
            mode_c = jnp.broadcast_to(mode[:, c:c + 1], (MODES, LANES))
            hi, lo = split(mode_c * jnp.exp(-rate_c * (lane16 + 1.0)))
            colw[pl.ds(c * MODES, MODES), :] = rate_c
            quad, at = c // 4, c % 4
            cols = pl.ds(at * LANES, LANES)
            lquad[quad, pl.ds(at * MODES, MODES), cols] = hi
            lquad[quad, pl.ds(64 + at * MODES, MODES), cols] = hi
            lquad[quad, pl.ds(128 + 64 * (quad % 2) + at * MODES, MODES), cols] = lo
        row_at = lax.broadcasted_iota(jnp.int32, (LANES, LANES), 0)
        lane_at = lax.broadcasted_iota(jnp.int32, (LANES, LANES), 1)
        behind = (LANES - 1 - row_at).astype(F32)
        keep = lane_at >= row_at

        def operators(g, _):
            start = pl.multiple_of(g * LANES, LANES)
            rate_row = jnp.transpose(colw[pl.ds(start, LANES), :])
            step_rate[g] = rate_row[:8, :] * LANES
            decays = jnp.exp(-rate_row * behind)
            e_hi, e_lo = split(decays)
            grown = quad_operands(jnp.exp(rate_row * (row_at + 1).astype(F32)))
            for half in range(2):
                kernels = jnp.dot(grown[half], lquad[g * 2 + half], preferred_element_type=F32)
                for at in range(4):
                    inner = jnp.where(keep, kernels[:, at * LANES:(at + 1) * LANES], 0.0)
                    t_hi, t_lo = split(inner)
                    c_in = half * 4 + at
                    mine = (lane_at >= c_in * MODES) & (lane_at < (c_in + 1) * MODES)
                    zero = jnp.zeros((LANES, LANES), F32)
                    m_hi = jnp.where(mine, e_hi.astype(F32), zero).astype(BF16)
                    m_lo = jnp.where(mine, e_lo.astype(F32), zero).astype(BF16)
                    c = g * 8 + c_in
                    weights[c, pl.ds(0, LANES), :] = jnp.concatenate([t_hi, m_hi], axis=1)
                    weights[c, pl.ds(LANES, LANES), :] = jnp.concatenate([t_lo, m_lo], axis=1)
            return 0

        lax.fori_loop(0, 4, operators, 0)

        for s in range(STREAMS):
            moved = pltpu.roll(filt[s], turn, 1)
            columns = jnp.transpose(jnp.concatenate([moved, jnp.zeros((LANES - TAPS, LANES), F32)], axis=0))
            for j in range(TAPS):
                taps[s * TAPS + j] = jnp.broadcast_to(columns[:CHANNELS, j:j + 1], (CHANNELS, LANES))

    gained()
    project(1, True)
    project(2, False)
    enter()
    sib = {1: send_sibling(1), 2: send_sibling(2)}
    send_ids()
    cross = {1: send_across(1, sib[1])}
    project(0, False)
    sib[0] = send_sibling(0)
    cross[2] = send_across(2, sib[2])
    cross[0] = send_across(0, sib[0])
    energies()
    for peer in peers_tp:
        energy_to(peer).start()
    prepare()
    each_other(0, known, lambda m: ids_to(m).wait_send())
    for copy in list(sib.values()) + [energy_to(peer) for peer in peers_tp]:
        copy.wait_send()

    row_of = lax.broadcasted_iota(jnp.int32, (HALF, LANES), 0)

    def mark(m):
        low = jnp.broadcast_to(ids[m] & (HALF - 1), (HALF, LANES))
        onehot[at(m)] = jnp.where(row_of == low, 1.0, 0.0).astype(BF16)

    def arrive(m):
        ids_from(m).wait_recv()
        mark(m)

    def mark_all(amount):
        def one(m, _):
            mark(m)
            return 0

        lax.fori_loop(0, amount, one, 0)

    mark(me)

    @pl.when(first)
    def _():
        each_other(0, quarter, arrive)
        pl.semaphore_wait(here.at[1], 1)
        piece_to(1).start()

    @pl.when(early)
    def _():
        each_other(quarter, half, arrive)

    @pl.when(first)
    def _():
        for later in (2, 3):
            pl.semaphore_wait(here.at[later], 1)
            piece_to(later).start()

    @pl.when(second)
    def _():
        in_one_piece(quarter, 1, leader).wait_recv()
        mark_all(quarter)

    for peer in peers_tp:
        energy_from(peer).wait_recv()
    scale = lax.rsqrt((en_all[0] + en_all[1] + en_all[2] + en_all[3]) / model_width + 1e-05)

    def tabulate(s, place, table):
        cross[s].wait_recv()
        height = table.shape[0] // 2
        for q in range(4):
            lanes = pl.ds(q * LANES, LANES)
            value = (own[s, :, lanes] + recv2[s, :, lanes]) * scale[q:q + 1, :]
            table[pl.ds((q // 2) * height + place * CHANNELS, CHANNELS), pl.ds((q % 2) * LANES, LANES)] = value.astype(BF16)

    tabulate(1, 0, tblkv)
    tabulate(2, 1, tblkv)
    each_other(half, seq_count, arrive)

    @pl.when(late)
    def _():
        in_one_piece(half, group, leader).wait_recv()
        mark_all(half)

    def filter_streams(table, streams, emit):
        height = table.shape[0] // 2
        lane = lax.broadcasted_iota(jnp.int32, (height, LANES), 1)
        first_lane = lane < 1
        first_two = lane < 2

        def pair(i, carry):
            before1, before2 = carry
            hot = jnp.concatenate([onehot[2 * i], onehot[2 * i + 1]], axis=1)
            both = jnp.dot(table[...], hot, preferred_element_type=F32)
            for u in range(2):
                j = 2 * i + u
                upper = jnp.broadcast_to(ids[place_of(j)], (height, LANES)) >= HALF
                lanes = slice(u * LANES, (u + 1) * LANES)
                now = jnp.where(upper, both[height:, lanes], both[:height, lanes])
                one, two = pltpu.roll(now, 1, 1), pltpu.roll(now, 2, 1)
                back1 = jnp.where(first_lane, before1, one)
                back2 = jnp.where(first_two, before2, two)
                before1, before2 = one, two
                filtered = []
                for place, s in enumerate(streams):
                    mine = slice(place * CHANNELS, (place + 1) * CHANNELS)
                    filtered.append(
                        taps[s * TAPS] * now[mine] + taps[s * TAPS + 1] * back1[mine] + taps[s * TAPS + 2] * back2[mine]
                    )
                emit(pl.ds(pl.multiple_of(j * CHANNELS, CHANNELS), CHANNELS), *filtered)
            return before1, before2

        nothing = jnp.zeros((height, LANES), F32)
        lax.fori_loop(0, seq_count // 2, pair, (nothing, nothing), unroll=seq_count // 2)

    def emit_gated(at, k, v):
        gated[at, :] = (k * v).astype(BF16).astype(F32)

    def emit_query(at, q):
        qfilt[at, :] = q

    filter_streams(tblkv, (1, 2), emit_gated)
    tabulate(0, 0, tblq)
    filter_streams(tblq, (0,), emit_query)

    def inside(g, _):
        total = jnp.zeros((seq_count, LANES), F32)
        for at in range(8):
            c = g * 8 + at
            x = gated[pl.ds(c, seq_count, stride=CHANNELS), :].astype(BF16)
            result = jnp.dot(jnp.concatenate([x, x], axis=1), weights[c], preferred_element_type=F32)
            yintra[c] = result[:, :LANES]
            total = total + result[:, LANES:]
        ends[g] = total
        return 0

    lax.fori_loop(0, 4, inside, 0, unroll=4)

    sub = lax.broadcasted_iota(jnp.int32, (8, LANES), 0)
    for g in range(4):
        rate_row = step_rate[g]
        own_decay = jnp.exp(-rate_row * sub.astype(F32))
        eighth = jnp.exp(-rate_row * 8.0)
        factors = [(d, jnp.where(sub >= d, jnp.exp(-rate_row * float(d)), 0.0)) for d in (1, 2, 4)]
        entering = jnp.zeros((8, LANES), F32)
        for v in range(seq_count // 8):
            span = ends[g, pl.ds(v * 8, 8), :]
            for d, factor in factors:
                span = span + factor * pltpu.roll(span, d, 0)
            shifted = jnp.where(sub >= 1, pltpu.roll(span, 1, 0), 0.0)
            carries[g, pl.ds(v * 8, 8), :] = shifted + own_decay * entering
            entering = jnp.broadcast_to(span[7:8, :], (8, LANES)) + eighth * entering

    def across(g, _):
        operands = quad_operands(carries[g])
        for half in range(2):
            result = jnp.dot(operands[half], lquad[g * 2 + half], preferred_element_type=F32)
            for at in range(4):
                c = g * 8 + half * 4 + at
                ybuf[pl.ds(c, seq_count, stride=CHANNELS), :] = yintra[c] + result[:, at * LANES:(at + 1) * LANES]
        return 0

    lax.fori_loop(0, 4, across, 0, unroll=4)

    def gate(j, _):
        at = pl.ds(pl.multiple_of(j * CHANNELS, CHANNELS), CHANNELS)
        obuf[:, pl.ds(pl.multiple_of(j * LANES, LANES), LANES)] = (qfilt[at, :] * ybuf[at, :]).astype(BF16)
        return 0

    lax.fori_loop(0, seq_count, gate, 0, unroll=8)


    @pl.when(first)
    def _():
        for later in (1, 2, 3):
            piece_to(later).wait_send()

    for copy in cross.values():
        copy.wait_send()


def on_device(token_ids, embedding, norm_gain, projection, short_filter, residues, decay_rates):
    seq_count = lax.axis_size("seq")
    vocab, features = embedding.shape
    model_width = short_filter.shape[2]
    tokens = seq_count * LANES
    hbm = pl.BlockSpec(memory_space=pltpu.HBM)
    dma = pltpu.SemaphoreType.DMA
    vmem = pltpu.VMEM
    scratch = [
        vmem((vocab, features), BF16),
        vmem((features // LANES, LANES), F32),
        vmem((STREAMS, features, LANES), BF16),
        vmem((seq_count, 1, LANES), jnp.int32),
        vmem((STREAMS, TAPS, LANES), F32),
        vmem((MODES, LANES), F32),
        vmem((MODES, LANES), F32),
        vmem((features, LANES), F32),
        vmem((STREAMS, features, 2 * LANES), BF16),
        vmem((STREAMS, 2, 2, CHANNELS, vocab), F32),
        vmem((STREAMS, 2, CHANNELS, vocab), F32),
        vmem((STREAMS, CHANNELS, vocab), F32),
        vmem((STREAMS, CHANNELS, vocab), F32),
        vmem((STREAMS, CHANNELS, vocab), F32),
        vmem((4, 4, LANES), F32),
        vmem((4 * CHANNELS, HALF), BF16),
        vmem((2 * CHANNELS, HALF), BF16),
        vmem((seq_count, HALF, LANES), BF16),
        vmem((STREAMS * TAPS, CHANNELS, LANES), F32),
        vmem((CHANNELS, 2 * LANES, 2 * LANES), BF16),
        vmem((8, 2 * LANES, 4 * LANES), BF16),
        vmem((CHANNELS * MODES, LANES), F32),
        vmem((4, 8, LANES), F32),
        vmem((seq_count * CHANNELS, LANES), F32),
        vmem((seq_count * CHANNELS, LANES), F32),
        vmem((CHANNELS, seq_count, LANES), F32),
        vmem((4, seq_count, LANES), F32),
        vmem((4, seq_count, LANES), F32),
        vmem((seq_count * CHANNELS, LANES), F32),
        dma((12,)),
        dma((seq_count,)),
        dma((seq_count,)),
        dma((STREAMS,)),
        dma((STREAMS,)),
        dma((STREAMS,)),
        dma((STREAMS,)),
        dma((4,)),
        dma((4,)),
        dma((4,)),
        dma((4,)),
        pltpu.SemaphoreType.REGULAR((4,)),
    ]
    return pl.pallas_call(
        functools.partial(kernel, model_width, seq_count),
        out_shape=vmem((CHANNELS, tokens), BF16),
        in_specs=[hbm] * 7,
        out_specs=pl.BlockSpec(memory_space=vmem),
        scratch_shapes=scratch,
        compiler_params=pltpu.CompilerParams(
            collective_id=0, has_side_effects=True, vmem_limit_bytes=56 * 1024 * 1024
        ),
    )(
        embedding,
        norm_gain.reshape(features // LANES, LANES),
        jnp.transpose(projection, (1, 0, 2)),
        token_ids.reshape(1, LANES),
        short_filter,
        jnp.transpose(residues),
        jnp.transpose(decay_rates),
    )


def solution(mesh):
    return jax.shard_map(
        on_device,
        mesh=mesh,
        in_specs=(P("seq"), P(None, "tp"), P("tp"), P("tp", None, "seq"), P(), P(), P()),
        out_specs=P(("seq", "tp"), None),
        check_vma=False,
    )
```

```python
import functools
import math

import jax
import jax.numpy as jnp
from jax import lax
from jax.experimental import pallas as pl
from jax.experimental.pallas import tpu as pltpu
from jax.sharding import PartitionSpec as P

MESH = pl.DeviceIdType.MESH
F32 = jnp.float32
BF16 = jnp.bfloat16
LANES = 128
CHANNELS = 32
MODES = 16
STREAMS = 3
TAPS = 3
VOCAB = 512
HALF = 256
ORDER = (1, 2, 0)


def split(x):
    hi = x.astype(BF16)
    return hi, (x - hi.astype(F32)).astype(BF16)


def quad_operands(x):
    hi = x.astype(BF16).astype(F32)
    lo = x - hi
    lane = lax.broadcasted_iota(jnp.int32, x.shape, 1)
    low = lane < 64
    first = jnp.where(low, hi, pltpu.roll(lo, 64, 1))
    second = jnp.where(low, pltpu.roll(hi, 64, 1), lo)
    hi = hi.astype(BF16)
    return (
        jnp.concatenate([first.astype(BF16), hi], axis=1),
        jnp.concatenate([second.astype(BF16), hi], axis=1),
    )


def kernel(
    model_width,
    seq_count,
    emb_hbm,
    gain_hbm,
    proj_hbm,
    ids_hbm,
    filt_hbm,
    res_hbm,
    rate_hbm,
    obuf,
    emb,
    gain,
    proj,
    ids,
    filt,
    res,
    rate,
    column,
    wproj,
    part,
    recv1,
    own,
    send2,
    recv2,
    en_all,
    tblkv,
    tblq,
    onehot,
    taps,
    weights,
    lquad,
    colw,
    step_rate,
    gated,
    qfilt,
    yintra,
    ends,
    carries,
    ybuf,
    load_sem,
    id_send,
    id_recv,
    s1_send,
    s1_recv,
    s2_send,
    s2_recv,
    e_send,
    e_recv,
    piece_send,
    piece_recv,
    here,
):
    seq = lax.axis_index("seq")
    tp = lax.axis_index("tp")
    core = lax.rem(tp, 2)
    far = tp // 2
    sibling = tp + 1 - 2 * core
    across_tp = lax.rem(tp + 2, 4)
    diagonal = lax.rem(sibling + 2, 4)
    peers_tp = (sibling, across_tp, diagonal)

    plane = 2 * max(seq_count // 16, 1)
    half = seq_count // 2

    def at(m):
        within = lax.rem(m, plane)
        return (within // 2) * 16 + (m // plane) * 2 + lax.rem(within, 2)

    def place_of(block):
        return lax.rem(block // 2, 8) * plane + (block // 16) * 2 + lax.rem(block, 2)

    me = place_of(seq)
    quarter = seq_count // 4
    first = me < quarter
    early = me < half
    second = jnp.logical_and(early, jnp.logical_not(first))
    late = jnp.logical_not(early)
    known = jnp.where(first, quarter, jnp.where(early, half, seq_count))
    first_greeted = jnp.where(first, 0, jnp.where(early, quarter, half))
    group = me // quarter
    leader = at(lax.rem(me, quarter))

    def each_other(first, last, act):
        def one(m, _):
            @pl.when(m != me)
            def _():
                act(m)

            return 0

        lax.fori_loop(first, last, one, 0)

    rows = emb_hbm.shape[0] // 4
    chan0 = pl.multiple_of(seq * LANES, LANES)
    loads = {}

    def load(name, slot, src, dst):
        loads[name] = pltpu.make_async_copy(src, dst, load_sem.at[slot])
        loads[name].start()

    load("gain", 1, gain_hbm, gain)
    for slot, name in enumerate(ORDER):
        load(f"proj{name}", 2 + slot, proj_hbm.at[name], proj.at[name])
    for r in range(4):
        load(f"emb{r}", 5 + r, emb_hbm.at[pl.ds(r * rows, rows), :], emb.at[pl.ds(r * rows, rows), :])
    load("ids", 0, ids_hbm, ids.at[me])
    load("rate", 9, rate_hbm.at[:, pl.ds(chan0, LANES)], rate)
    load("res", 10, res_hbm.at[:, pl.ds(chan0, LANES)], res)
    load("filt", 11, filt_hbm.at[:, :, pl.ds(chan0, LANES)], filt)

    barrier = pltpu.get_barrier_semaphore()

    def greet(m):
        pl.semaphore_signal(barrier, inc=1, device_id={"seq": at(m), "tp": tp}, device_id_type=MESH)

    for peer in peers_tp:
        pl.semaphore_signal(barrier, inc=1, device_id={"seq": seq, "tp": peer}, device_id_type=MESH)
    each_other(first_greeted, seq_count, greet)

    def ids_to(m):
        return pltpu.make_async_remote_copy(
            src_ref=ids.at[me], dst_ref=ids.at[me],
            send_sem=id_send.at[m], recv_sem=id_recv.at[me],
            device_id={"seq": at(m), "tp": tp}, device_id_type=MESH,
        )

    def ids_from(m):
        return pltpu.make_async_remote_copy(
            src_ref=ids.at[m], dst_ref=ids.at[m],
            send_sem=id_send.at[m], recv_sem=id_recv.at[m],
            device_id={"seq": at(m), "tp": tp}, device_id_type=MESH,
        )

    def in_one_piece(amount, slot, peer):
        return pltpu.make_async_remote_copy(
            src_ref=ids.at[pl.ds(0, amount)], dst_ref=ids.at[pl.ds(0, amount)],
            send_sem=piece_send.at[slot], recv_sem=piece_recv.at[slot],
            device_id={"seq": peer, "tp": tp}, device_id_type=MESH,
        )

    def piece_to(later):
        return in_one_piece(quarter if later == 1 else half, later, at(lax.rem(me, quarter) + later * quarter))

    def gained():
        features = proj.shape[1]
        loads["gain"].wait()
        gain_rows = gain.shape[0]
        turned = jnp.transpose(
            jnp.concatenate([gain[...], jnp.zeros((LANES - gain_rows, LANES), F32)], axis=0)
        )
        for k in range(gain_rows):
            column[k * LANES:(k + 1) * LANES, :] = jnp.broadcast_to(turned[:, k:k + 1], (LANES, LANES))
        for s in ORDER:
            loads[f"proj{s}"].wait()

            def one(k, _):
                span = pl.ds(pl.multiple_of(k * LANES, LANES), LANES)
                hi, lo = split(proj[s, span, :].astype(F32) * column[span, :])
                wproj[s, span, :] = jnp.concatenate([hi, lo], axis=1)
                return 0

            lax.fori_loop(0, features // LANES, one, 0, unroll=math.gcd(4, features // LANES))

    def project(s, first):
        for r in range(4):
            if first:
                loads[f"emb{r}"].wait()
            block = emb[pl.ds(r * rows, rows), :]
            both = jnp.dot(block, wproj[s], preferred_element_type=F32)
            turned = jnp.transpose(both[:, :LANES] + both[:, LANES:])
            for q in range(4):
                piece = turned[q * CHANNELS:(q + 1) * CHANNELS, :]
                part[s, q % 2, q // 2, :, r * rows:(r + 1) * rows] = piece

    def send_sibling(s):
        copy = pltpu.make_async_remote_copy(
            src_ref=part.at[s, 1 - core], dst_ref=recv1.at[s],
            send_sem=s1_send.at[s], recv_sem=s1_recv.at[s],
            device_id={"seq": seq, "tp": sibling}, device_id_type=MESH,
        )
        copy.start()
        return copy

    def send_across(s, copy):
        copy.wait_recv()
        send2[s] = part[s, core, 1 - far] + recv1[s, 1 - far]
        after = pltpu.make_async_remote_copy(
            src_ref=send2.at[s], dst_ref=recv2.at[s],
            send_sem=s2_send.at[s], recv_sem=s2_recv.at[s],
            device_id={"seq": seq, "tp": across_tp}, device_id_type=MESH,
        )
        after.start()
        own[s] = part[s, core, far] + recv1[s, far]
        return after

    def energies():
        for r in range(4):
            block = emb[pl.ds(r * rows, rows), :]
            total = jnp.zeros((rows, LANES), F32)
            for k in range(emb.shape[1] // LANES):
                piece = block[:, k * LANES:(k + 1) * LANES].astype(F32)
                total = total + piece * piece
            en_all[tp, pl.ds(r, 1), :] = jnp.sum(jnp.transpose(total), axis=0, keepdims=True)

    def energy_to(peer):
        return pltpu.make_async_remote_copy(
            src_ref=en_all.at[tp], dst_ref=en_all.at[tp], send_sem=e_send.at[peer], recv_sem=e_recv.at[tp],
            device_id={"seq": seq, "tp": peer}, device_id_type=MESH,
        )

    def energy_from(peer):
        return pltpu.make_async_remote_copy(
            src_ref=en_all.at[peer], dst_ref=en_all.at[peer], send_sem=e_send.at[peer], recv_sem=e_recv.at[peer],
            device_id={"seq": seq, "tp": peer}, device_id_type=MESH,
        )

    def enter():
        loads["ids"].wait()
        pl.semaphore_wait(barrier, known + 2)

        @pl.when(jnp.logical_not(first))
        def _():
            pl.semaphore_signal(here.at[group], inc=1, device_id={"seq": leader, "tp": tp}, device_id_type=MESH)

    def send_ids():
        each_other(0, known, lambda m: ids_to(m).start())

    def prepare():
        loads["rate"].wait()
        loads["res"].wait()
        loads["filt"].wait()
        turn = lax.rem(LANES - tp * CHANNELS, LANES)
        rates = pltpu.roll(rate[...], turn, 1)
        twice = 2.0 * rates
        series = twice * (
            1.0 - twice / 2 * (1.0 - twice / 3 * (1.0 - twice / 4 * (1.0 - twice / 5 * (1.0 - twice / 6))))
        )
        lost = jnp.where(twice < 0.125, series, 1.0 - jnp.exp(-twice))
        mode = pltpu.roll(res[...], turn, 1) * jnp.sqrt(lost)
        lane16 = lax.broadcasted_iota(jnp.int32, (MODES, LANES), 1).astype(F32)
        lquad[...] = jnp.zeros(lquad.shape, BF16)
        for c in range(CHANNELS):
            rate_c = jnp.broadcast_to(rates[:, c:c + 1], (MODES, LANES))
            mode_c = jnp.broadcast_to(mode[:, c:c + 1], (MODES, LANES))
            hi, lo = split(mode_c * jnp.exp(-rate_c * (lane16 + 1.0)))
            colw[pl.ds(c * MODES, MODES), :] = rate_c
            quad, at = c // 4, c % 4
            cols = pl.ds(at * LANES, LANES)
            lquad[quad, pl.ds(at * MODES, MODES), cols] = hi
            lquad[quad, pl.ds(64 + at * MODES, MODES), cols] = hi
            lquad[quad, pl.ds(128 + 64 * (quad % 2) + at * MODES, MODES), cols] = lo
        row_at = lax.broadcasted_iota(jnp.int32, (LANES, LANES), 0)
        lane_at = lax.broadcasted_iota(jnp.int32, (LANES, LANES), 1)
        behind = (LANES - 1 - row_at).astype(F32)
        keep = lane_at >= row_at

        def operators(g, _):
            start = pl.multiple_of(g * LANES, LANES)
            rate_row = jnp.transpose(colw[pl.ds(start, LANES), :])
            step_rate[g] = rate_row[:8, :] * LANES
            decays = jnp.exp(-rate_row * behind)
            e_hi, e_lo = split(decays)
            grown = quad_operands(jnp.exp(rate_row * (row_at + 1).astype(F32)))
            for half in range(2):
                kernels = jnp.dot(grown[half], lquad[g * 2 + half], preferred_element_type=F32)
                for at in range(4):
                    inner = jnp.where(keep, kernels[:, at * LANES:(at + 1) * LANES], 0.0)
                    t_hi, t_lo = split(inner)
                    c_in = half * 4 + at
                    mine = (lane_at >= c_in * MODES) & (lane_at < (c_in + 1) * MODES)
                    zero = jnp.zeros((LANES, LANES), F32)
                    m_hi = jnp.where(mine, e_hi.astype(F32), zero).astype(BF16)
                    m_lo = jnp.where(mine, e_lo.astype(F32), zero).astype(BF16)
                    c = g * 8 + c_in
                    weights[c, pl.ds(0, LANES), :] = jnp.concatenate([t_hi, m_hi], axis=1)
                    weights[c, pl.ds(LANES, LANES), :] = jnp.concatenate([t_lo, m_lo], axis=1)
            return 0

        lax.fori_loop(0, 4, operators, 0)

        for s in range(STREAMS):
            moved = pltpu.roll(filt[s], turn, 1)
            columns = jnp.transpose(jnp.concatenate([moved, jnp.zeros((LANES - TAPS, LANES), F32)], axis=0))
            for j in range(TAPS):
                taps[s * TAPS + j] = jnp.broadcast_to(columns[:CHANNELS, j:j + 1], (CHANNELS, LANES))

    gained()
    project(1, True)
    project(2, False)
    enter()
    sib = {1: send_sibling(1), 2: send_sibling(2)}
    send_ids()
    cross = {1: send_across(1, sib[1])}
    project(0, False)
    sib[0] = send_sibling(0)
    cross[2] = send_across(2, sib[2])
    cross[0] = send_across(0, sib[0])
    energies()
    for peer in peers_tp:
        energy_to(peer).start()
    prepare()
    each_other(0, known, lambda m: ids_to(m).wait_send())
    for copy in list(sib.values()) + [energy_to(peer) for peer in peers_tp]:
        copy.wait_send()

    row_of = lax.broadcasted_iota(jnp.int32, (HALF, LANES), 0)

    def mark(m):
        low = jnp.broadcast_to(ids[m] & (HALF - 1), (HALF, LANES))
        onehot[at(m)] = jnp.where(row_of == low, 1.0, 0.0).astype(BF16)

    def arrive(m):
        ids_from(m).wait_recv()
        mark(m)

    def mark_all(amount):
        def one(m, _):
            mark(m)
            return 0

        lax.fori_loop(0, amount, one, 0)

    mark(me)

    @pl.when(first)
    def _():
        each_other(0, quarter, arrive)
        pl.semaphore_wait(here.at[1], 1)
        piece_to(1).start()

    @pl.when(early)
    def _():
        each_other(quarter, half, arrive)

    @pl.when(first)
    def _():
        for later in (2, 3):
            pl.semaphore_wait(here.at[later], 1)
            piece_to(later).start()

    @pl.when(second)
    def _():
        in_one_piece(quarter, 1, leader).wait_recv()
        mark_all(quarter)

    for peer in peers_tp:
        energy_from(peer).wait_recv()
    scale = lax.rsqrt((en_all[0] + en_all[1] + en_all[2] + en_all[3]) / model_width + 1e-05)

    def tabulate(s, place, table):
        cross[s].wait_recv()
        height = table.shape[0] // 2
        for q in range(4):
            lanes = pl.ds(q * LANES, LANES)
            value = (own[s, :, lanes] + recv2[s, :, lanes]) * scale[q:q + 1, :]
            table[pl.ds((q // 2) * height + place * CHANNELS, CHANNELS), pl.ds((q % 2) * LANES, LANES)] = value.astype(BF16)

    tabulate(1, 0, tblkv)
    tabulate(2, 1, tblkv)
    each_other(half, seq_count, arrive)

    @pl.when(late)
    def _():
        in_one_piece(half, group, leader).wait_recv()
        mark_all(half)

    def filter_streams(table, streams, emit):
        height = table.shape[0] // 2
        lane = lax.broadcasted_iota(jnp.int32, (height, LANES), 1)
        first_lane = lane < 1
        first_two = lane < 2

        def pair(i, carry):
            before1, before2 = carry
            hot = jnp.concatenate([onehot[2 * i], onehot[2 * i + 1]], axis=1)
            both = jnp.dot(table[...], hot, preferred_element_type=F32)
            for u in range(2):
                j = 2 * i + u
                upper = jnp.broadcast_to(ids[place_of(j)], (height, LANES)) >= HALF
                lanes = slice(u * LANES, (u + 1) * LANES)
                now = jnp.where(upper, both[height:, lanes], both[:height, lanes])
                one, two = pltpu.roll(now, 1, 1), pltpu.roll(now, 2, 1)
                back1 = jnp.where(first_lane, before1, one)
                back2 = jnp.where(first_two, before2, two)
                before1, before2 = one, two
                filtered = []
                for place, s in enumerate(streams):
                    mine = slice(place * CHANNELS, (place + 1) * CHANNELS)
                    filtered.append(
                        taps[s * TAPS] * now[mine] + taps[s * TAPS + 1] * back1[mine] + taps[s * TAPS + 2] * back2[mine]
                    )
                emit(pl.ds(pl.multiple_of(j * CHANNELS, CHANNELS), CHANNELS), *filtered)
            return before1, before2

        nothing = jnp.zeros((height, LANES), F32)
        lax.fori_loop(0, seq_count // 2, pair, (nothing, nothing), unroll=seq_count // 2)

    def emit_gated(at, k, v):
        gated[at, :] = (k * v).astype(BF16).astype(F32)

    def emit_query(at, q):
        qfilt[at, :] = q

    filter_streams(tblkv, (1, 2), emit_gated)
    tabulate(0, 0, tblq)
    filter_streams(tblq, (0,), emit_query)

    def inside(g, _):
        total = jnp.zeros((seq_count, LANES), F32)
        for at in range(8):
            c = g * 8 + at
            x = gated[pl.ds(c, seq_count, stride=CHANNELS), :].astype(BF16)
            result = jnp.dot(jnp.concatenate([x, x], axis=1), weights[c], preferred_element_type=F32)
            yintra[c] = result[:, :LANES]
            total = total + result[:, LANES:]
        ends[g] = total
        return 0

    lax.fori_loop(0, 4, inside, 0, unroll=4)

    sub = lax.broadcasted_iota(jnp.int32, (8, LANES), 0)
    for g in range(4):
        rate_row = step_rate[g]
        own_decay = jnp.exp(-rate_row * sub.astype(F32))
        eighth = jnp.exp(-rate_row * 8.0)
        factors = [(d, jnp.where(sub >= d, jnp.exp(-rate_row * float(d)), 0.0)) for d in (1, 2, 4)]
        entering = jnp.zeros((8, LANES), F32)
        for v in range(seq_count // 8):
            span = ends[g, pl.ds(v * 8, 8), :]
            for d, factor in factors:
                span = span + factor * pltpu.roll(span, d, 0)
            shifted = jnp.where(sub >= 1, pltpu.roll(span, 1, 0), 0.0)
            carries[g, pl.ds(v * 8, 8), :] = shifted + own_decay * entering
            entering = jnp.broadcast_to(span[7:8, :], (8, LANES)) + eighth * entering

    def across(g, _):
        operands = quad_operands(carries[g])
        for half in range(2):
            result = jnp.dot(operands[half], lquad[g * 2 + half], preferred_element_type=F32)
            for at in range(4):
                c = g * 8 + half * 4 + at
                ybuf[pl.ds(c, seq_count, stride=CHANNELS), :] = yintra[c] + result[:, at * LANES:(at + 1) * LANES]
        return 0

    lax.fori_loop(0, 4, across, 0, unroll=4)

    def gate(j, _):
        at = pl.ds(pl.multiple_of(j * CHANNELS, CHANNELS), CHANNELS)
        obuf[:, pl.ds(pl.multiple_of(j * LANES, LANES), LANES)] = (qfilt[at, :] * ybuf[at, :]).astype(BF16)
        return 0

    lax.fori_loop(0, seq_count, gate, 0, unroll=8)


    @pl.when(first)
    def _():
        for later in (1, 2, 3):
            piece_to(later).wait_send()

    for copy in cross.values():
        copy.wait_send()


def on_device(token_ids, embedding, norm_gain, projection, short_filter, residues, decay_rates):
    seq_count = lax.axis_size("seq")
    vocab, features = embedding.shape
    model_width = short_filter.shape[2]
    tokens = seq_count * LANES
    hbm = pl.BlockSpec(memory_space=pltpu.HBM)
    dma = pltpu.SemaphoreType.DMA
    vmem = pltpu.VMEM
    scratch = [
        vmem((vocab, features), BF16),
        vmem((features // LANES, LANES), F32),
        vmem((STREAMS, features, LANES), BF16),
        vmem((seq_count, 1, LANES), jnp.int32),
        vmem((STREAMS, TAPS, LANES), F32),
        vmem((MODES, LANES), F32),
        vmem((MODES, LANES), F32),
        vmem((features, LANES), F32),
        vmem((STREAMS, features, 2 * LANES), BF16),
        vmem((STREAMS, 2, 2, CHANNELS, vocab), F32),
        vmem((STREAMS, 2, CHANNELS, vocab), F32),
        vmem((STREAMS, CHANNELS, vocab), F32),
        vmem((STREAMS, CHANNELS, vocab), F32),
        vmem((STREAMS, CHANNELS, vocab), F32),
        vmem((4, 4, LANES), F32),
        vmem((4 * CHANNELS, HALF), BF16),
        vmem((2 * CHANNELS, HALF), BF16),
        vmem((seq_count, HALF, LANES), BF16),
        vmem((STREAMS * TAPS, CHANNELS, LANES), F32),
        vmem((CHANNELS, 2 * LANES, 2 * LANES), BF16),
        vmem((8, 2 * LANES, 4 * LANES), BF16),
        vmem((CHANNELS * MODES, LANES), F32),
        vmem((4, 8, LANES), F32),
        vmem(((seq_count + 1) * CHANNELS, LANES), F32),
        vmem(((seq_count + 1) * CHANNELS, LANES), F32),
        vmem((CHANNELS, seq_count, LANES), F32),
        vmem((4, seq_count, LANES), F32),
        vmem((4, seq_count, LANES), F32),
        vmem(((seq_count + 1) * CHANNELS, LANES), F32),
        dma((12,)),
        dma((seq_count,)),
        dma((seq_count,)),
        dma((STREAMS,)),
        dma((STREAMS,)),
        dma((STREAMS,)),
        dma((STREAMS,)),
        dma((4,)),
        dma((4,)),
        dma((4,)),
        dma((4,)),
        pltpu.SemaphoreType.REGULAR((4,)),
    ]
    return pl.pallas_call(
        functools.partial(kernel, model_width, seq_count),
        out_shape=vmem((CHANNELS, tokens), BF16),
        in_specs=[hbm] * 7,
        out_specs=pl.BlockSpec(memory_space=vmem),
        scratch_shapes=scratch,
        compiler_params=pltpu.CompilerParams(
            collective_id=0, has_side_effects=True, vmem_limit_bytes=56 * 1024 * 1024
        ),
    )(
        embedding,
        norm_gain.reshape(features // LANES, LANES),
        jnp.transpose(projection, (1, 0, 2)),
        token_ids.reshape(1, LANES),
        short_filter,
        jnp.transpose(residues),
        jnp.transpose(decay_rates),
    )


def solution(mesh):
    return jax.shard_map(
        on_device,
        mesh=mesh,
        in_specs=(P("seq"), P(None, "tp"), P("tp"), P("tp", None, "seq"), P(), P(), P()),
        out_specs=P(("seq", "tp"), None),
        check_vma=False,
    )
```
